512 devices in a mesh: row: 64 (over z, x, core), col: 8 (over y).
Axes of the slice: x: 4, y: 8, z: 8, core: 2. Of those that a mesh axis runs over, the one named last changes fastest.
Arguments:
- tokens: bfloat16 [512, 8192], P('row', 'col'), may hold values from -6 to 6
- out_grad: bfloat16 [512, 8192], P('row', 'col'), may hold values from -6 to 6
- w_gate: bfloat16 [14336, 8192], P('row', 'col'), may hold values from -0.125 to 0.125
- w_up: bfloat16 [14336, 8192], P('row', 'col'), may hold values from -0.125 to 0.125
- w_down: bfloat16 [14336, 8192], P('row', 'col'), may hold values from -0.09375 to 0.09375
- mask_gate: int32 [112, 64], replicated, may hold values 0 or 1
- mask_up: int32 [112, 64], replicated, may hold values 0 or 1
- mask_down: int32 [112, 64], replicated, may hold values 0 or 1
Outputs:
- grad_tokens: bfloat16 [512, 8192], P('row', 'col')
- grad_gate: bfloat16 [14336, 8192], P('row', 'col')
- grad_up: bfloat16 [14336, 8192], P('row', 'col')
- grad_down: bfloat16 [14336, 8192], P('row', 'col')
The draws below stay inside these ranges and needn't reach their ends.
All inputs are finite; a program needn't handle non-finite values.
Results may differ from the reference program's by a relative error of at most 0.005.
Values may be sent and summed in bfloat16 or wider, within the bound.
A program may use at most 64 MiB of HBM per device.

```python
import jax
import jax.numpy as jnp

D = 8192
FF = 14336
BLOCK = 128
TOKENS = 512


def plant(result, key, low, high):
    extent = result.shape
    spot = [jax.random.randint(jax.random.fold_in(key, axis), (), 0, extent[axis]) for axis in range(len(extent))]
    result = result.at[tuple(spot)].set(low)
    longest = extent.index(max(extent))
    spot[longest] = (spot[longest] + 1) % extent[longest]
    return result.at[tuple(spot)].set(high)


def shard_levels(own_key, dims, cuts, low, top_value):
    def one(dim, shards_of):
        steps = jax.random.uniform(jax.random.fold_in(jax.random.fold_in(own_key, 6), dim), (shards_of,), jnp.float32, low / len(cuts), top_value / len(cuts))
        return jnp.repeat(jnp.exp(steps), dims[dim] // shards_of).reshape((-1,) + (1,) * (len(dims) - dim - 1))

    factor_of = one(*cuts[0])
    for cut in cuts[1:]:
        factor_of = factor_of * one(*cut)
    return factor_of


def centred(stream_key, extent, deviation, limit, pieces=(), kind=jnp.bfloat16):
    entries = jax.random.normal(stream_key, extent, jnp.float32) * deviation
    if len(pieces) > 0:
        entries = shard_levels(stream_key, extent, pieces, -0.22, 0.18) * entries
    return jnp.clip(entries, min=-limit, max=limit).astype(kind)


def setup_inputs(seed: int = 0) -> dict:
    streams_of = jax.random.split(jax.random.key(seed), 9)
    return {
        "tokens": centred(streams_of[0], (TOKENS, D), 1.0, 6.0, ((0, 64), (1, 8))),
        "out_grad": centred(streams_of[1], (TOKENS, D), 1.0, 6.0, ((0, 64), (1, 8))),
        "w_gate": centred(streams_of[2], (FF, D), (D // 4) ** -0.5, 0.125, ((0, 64), (1, 8))),
        "w_up": centred(streams_of[3], (FF, D), (D // 4) ** -0.5, 0.125, ((0, 64), (1, 8))),
        "w_down": centred(streams_of[4], (FF, D), (FF // 4) ** -0.5, 0.09375, ((0, 64), (1, 8))),
        "mask_gate": plant((jax.random.randint(streams_of[5], (FF // BLOCK, D // BLOCK), 0, 4) < 1).astype(jnp.int32), jax.random.fold_in(streams_of[5], 1), 0, 1),
        "mask_up": plant((jax.random.randint(streams_of[6], (FF // BLOCK, D // BLOCK), 0, 4) < 1).astype(jnp.int32), jax.random.fold_in(streams_of[6], 1), 0, 1),
        "mask_down": plant((jax.random.randint(streams_of[7], (FF // BLOCK, D // BLOCK), 0, 4) < 1).astype(jnp.int32), jax.random.fold_in(streams_of[7], 1), 0, 1),
    }


def widen(mask):
    grown = jnp.repeat(jnp.repeat(mask, BLOCK, axis=0), BLOCK, axis=1)
    return grown.astype(jnp.bfloat16)


def reference(tokens, out_grad, w_gate, w_up, w_down, mask_gate, mask_up, mask_down):
    keep_gate = widen(mask_gate)
    keep_up = widen(mask_up)
    keep_down = widen(mask_down)
    gate_eff = w_gate * keep_gate
    up_eff = w_up * keep_up
    down_eff = w_down * keep_down
    gate = jnp.dot(tokens, gate_eff.T, preferred_element_type=jnp.float32)
    upper = jnp.dot(tokens, up_eff.T, preferred_element_type=jnp.float32)
    dhidden = jnp.dot(out_grad, down_eff.T, preferred_element_type=jnp.float32)
    sig = jax.nn.sigmoid(gate)
    hidden = (gate * sig * upper).astype(jnp.bfloat16)
    dup = (dhidden * gate * sig).astype(jnp.bfloat16)
    dgate = (dhidden * upper * sig * (1.0 + gate * (1.0 - sig))).astype(jnp.bfloat16)
    grad_down = (jnp.dot(hidden.T, out_grad, preferred_element_type=jnp.float32) * keep_down.astype(jnp.float32)).astype(jnp.bfloat16)
    grad_gate = (jnp.dot(dgate.T, tokens, preferred_element_type=jnp.float32) * keep_gate.astype(jnp.float32)).astype(jnp.bfloat16)
    grad_up = (jnp.dot(dup.T, tokens, preferred_element_type=jnp.float32) * keep_up.astype(jnp.float32)).astype(jnp.bfloat16)
    grad_tokens = (jnp.dot(dgate, gate_eff, preferred_element_type=jnp.float32)
                   + jnp.dot(dup, up_eff, preferred_element_type=jnp.float32)).astype(jnp.bfloat16)
    return grad_tokens, grad_gate, grad_up, grad_down
```

```python
import jax
import jax.numpy as jnp
from jax import lax
from jax.experimental import pallas as pl
from jax.experimental.pallas import tpu as pltpu
from jax.sharding import PartitionSpec as P

BLOCK = 128
NZ, NX, NY = 8, 4, 8
UNITS, FEATS, PAD = 224, 1024, 256
WIDE = 3 * PAD
GROUPS = ((0, 1), (-1, 2), (-2, 3), (-3, 4))
F32, BF16 = jnp.float32, jnp.bfloat16


def expand(mask, row_start, col_start):
    blocks, wide = mask.shape
    unit = (row_start + lax.broadcasted_iota(jnp.int32, (UNITS, blocks), 0)) >> 7
    left = (unit == lax.broadcasted_iota(jnp.int32, (UNITS, blocks), 1)).astype(F32).astype(BF16)
    feat = (col_start + lax.broadcasted_iota(jnp.int32, (wide, FEATS), 1)) >> 7
    right = (feat == lax.broadcasted_iota(jnp.int32, (wide, FEATS), 0)).astype(F32).astype(BF16)
    inner = jnp.dot(left, mask.astype(F32).astype(BF16), preferred_element_type=F32)
    return jnp.dot(inner.astype(BF16), right, preferred_element_type=F32)


def kernel(
    tok, grd, wg, wu, wd, mg, mu, md,
    o_t, o_g, o_u, o_d,
    tokv, grdv, wv, mv, G, WE, KEEP, TOKS, GRDS, P32,
    SP, SM, S2, RP, RM, R2, SA, SB, RA, RB, D, GTS, GR, XS, XR, KX, ZS, ZR, ZO,
    lsem, xs_s, xs_r, z_s, z_r, c_s, c_r, y1_s, y1_r, y2_s, y2_r, d_s, d_r, e_s, e_r,
    g_s, g_r, h_s, h_r, k_s, k_r,
):
    row, y = lax.axis_index("row"), lax.axis_index("col")
    c = lax.rem(row, 2)
    x = lax.rem(row // 2, NX)
    z = row // (2 * NX)

    def zi(d):
        return lax.rem(z + (d + NZ), NZ)

    def xi(d):
        return lax.rem(x + (d + NX), NX)

    def yi(d):
        return lax.rem(y + (d + NY), NY)

    def dev(dz=0, dx=0, dc=0, dy=0):
        return ((zi(dz) * NX + xi(dx)) * 2 + lax.rem(c + dc, 2), yi(dy))

    sends = []

    def send(src, dst, ssem, rsem, where):
        cp = pltpu.make_async_remote_copy(
            src, dst, ssem, rsem, device_id=where, device_id_type=pl.DeviceIdType.MESH
        )
        cp.start()
        sends.append(cp)

    def arrived(dst, ssem, rsem):
        pltpu.make_async_remote_copy(
            dst, dst, ssem, rsem, device_id=dev(dc=1), device_id_type=pl.DeviceIdType.MESH
        ).wait_recv()

    peers = (
        [dev(dc=1)]
        + [dev(dx=k) for k in (1, 2, 3)]
        + [dev(dz=k) for k in (1, 2, 3, 4, 5, 6, 7)]
        + [dev(dy=k) for k in (1, 2, -1, -2)]
    )
    barrier = pltpu.get_barrier_semaphore()
    for p in peers:
        pl.semaphore_signal(barrier, inc=1, device_id=p, device_id_type=pl.DeviceIdType.MESH)
    loads = [
        pltpu.make_async_copy(s, d, lsem.at[i])
        for i, (s, d) in enumerate(
            (
                (tok, tokv), (grd, grdv),
                (mg, mv.at[0]), (mu, mv.at[1]), (md, mv.at[2]),
                (wg, wv.at[0]), (wu, wv.at[1]), (wd, wv.at[2]),
            )
        )
    ]
    for cp in loads:
        cp.start()
    loads[0].wait()
    loads[1].wait()
    G[z, c, x] = jnp.concatenate([tokv[...].astype(F32), grdv[...].astype(F32)], axis=0).astype(BF16)
    pl.semaphore_wait(barrier, len(peers))

    def block(dz, b):
        return G.at[zi(dz), c, xi(-b)]

    def along_z(way, hop, b):
        ref = block(-way * (hop - 1), b)
        i = 0 if way > 0 else 1
        send(ref, ref, z_s.at[i, hop - 1, b], z_r.at[i, hop - 1, b], dev(dz=way))

    def from_z(way, hop, b):
        i = 0 if way > 0 else 1
        arrived(block(-way * hop, b), z_s.at[i, hop - 1, b], z_r.at[i, hop - 1, b])

    def to_core(dz):
        ref = G.at[zi(dz), c]
        send(ref, ref, c_s.at[dz + 3], c_r.at[dz + 3], dev(dc=1))

    def from_core(dz):
        arrived(G.at[zi(dz), 1 - c], c_s.at[dz + 3], c_r.at[dz + 3])

    own = block(0, 0)
    along_z(1, 1, 0)
    along_z(-1, 1, 0)
    for b in (1, 3, 2):
        send(own, own, xs_s.at[b - 1], xs_r.at[b - 1], dev(dx=b))

    for i in range(3):
        loads[2 + i].wait()
        loads[5 + i].wait()
        keep = expand(mv[i], row * UNITS, y * FEATS)
        KEEP[i] = keep.astype(BF16)
        WE[i, :UNITS] = (wv[i].astype(F32) * keep).astype(BF16)
        WE[i, UNITS:] = jnp.zeros((PAD - UNITS, FEATS), BF16)

    for b in (1, 3, 2):
        arrived(block(0, b), xs_s.at[b - 1], xs_r.at[b - 1])
        along_z(1, 1, b)
        along_z(-1, 1, b)
    to_core(0)

    def goes(way, hop, b):
        return hop <= 3 or (hop == 4 and (b < 2) == (way > 0))

    def ring(hop):
        for b in (0, 1, 3, 2):
            for way in (-1, 1):
                if goes(way, hop, b):
                    from_z(way, hop, b)
                    if goes(way, hop + 1, b) and hop < 4:
                        along_z(way, hop + 1, b)
        if hop < 4:
            to_core(hop)
            to_core(-hop)
        else:
            to_core(4)

    def partial(g):
        toks, grds = [], []
        for d in GROUPS[g]:
            from_core(d)
            v = G[zi(d)].astype(F32)
            toks.append(v[:, :, :8].reshape(64, FEATS))
            grds.append(v[:, :, 8:].reshape(64, FEATS))
        t = jnp.concatenate(toks, axis=0).astype(BF16)
        r = jnp.concatenate(grds, axis=0).astype(BF16)
        TOKS[g * 128 : g * 128 + 128] = t
        GRDS[g * 128 : g * 128 + 128] = r
        nt = (((1,), (1,)), ((), ()))
        for i, v in enumerate((t, t, r)):
            P32[g, :, :, i * PAD : (i + 1) * PAD] = lax.dot_general(
                v, WE[i], nt, preferred_element_type=F32
            ).reshape(NY, 16, PAD)
        SP[g, 0] = P32[g, yi(1)].astype(BF16)
        SP[g, 1] = P32[g, yi(3)].astype(BF16)
        send(SP.at[g], RP.at[g], y1_s.at[g, 0], y1_r.at[g, 0], dev(dy=1))
        SM[g, 0] = P32[g, yi(-1)].astype(BF16)
        SM[g, 1] = P32[g, yi(-3)].astype(BF16)
        send(SM.at[g], RM.at[g], y1_s.at[g, 1], y1_r.at[g, 1], dev(dy=-1))
        S2[g] = P32[g, yi(4)].astype(BF16)
        send(S2.at[g], R2.at[g], y1_s.at[g, 2], y1_r.at[g, 2], dev(dy=2 if g % 2 == 0 else -2))

    def relay(g):
        arrived(RP.at[g], y1_s.at[g, 0], y1_r.at[g, 0])
        arrived(RM.at[g], y1_s.at[g, 1], y1_r.at[g, 1])
        arrived(R2.at[g], y1_s.at[g, 2], y1_r.at[g, 2])
        up = P32[g, yi(2)] + RP[g, 1].astype(F32)
        down = P32[g, yi(-2)] + RM[g, 1].astype(F32)
        far = R2[g].astype(F32)
        if g % 2 == 0:
            up = up + far
        else:
            down = down + far
        SB[g] = up.astype(BF16)
        send(SB.at[g], RB.at[g], y2_s.at[g, 0], y2_r.at[g, 0], dev(dy=2))
        SA[g] = down.astype(BF16)
        send(SA.at[g], RA.at[g], y2_s.at[g, 1], y2_r.at[g, 1], dev(dy=-2))

    def owned(g):
        arrived(RB.at[g], y2_s.at[g, 0], y2_r.at[g, 0])
        arrived(RA.at[g], y2_s.at[g, 1], y2_r.at[g, 1])
        total = (
            P32[g, y]
            + (RP[g, 0].astype(F32) + RM[g, 0].astype(F32))
            + (RB[g].astype(F32) + RA[g].astype(F32))
        )
        gate, upper, dhid = total[:, :PAD], total[:, PAD : 2 * PAD], total[:, 2 * PAD :]
        sig = jax.nn.sigmoid(gate)
        act = gate * sig
        hidden = act * upper
        dup = dhid * act
        dgate = dhid * upper * sig * (1.0 + gate * (1.0 - sig))
        D[g, y] = jnp.concatenate([hidden, dgate, dup], axis=1).astype(BF16)
        ref = D.at[g, y]
        for i, k in enumerate((2, -2, 1, -1)):
            send(ref, ref, d_s.at[g, i], d_r.at[g, i], dev(dy=k))

    def spread(g):
        low, high = D.at[g, yi(-2)], D.at[g, yi(2)]
        arrived(low, d_s.at[g, 0], d_r.at[g, 0])
        send(low, low, e_s.at[g, 0], e_r.at[g, 0], dev(dy=1))
        if g % 2 == 0:
            send(low, low, e_s.at[g, 2], e_r.at[g, 2], dev(dy=2))
        arrived(high, d_s.at[g, 1], d_r.at[g, 1])
        send(high, high, e_s.at[g, 1], e_r.at[g, 1], dev(dy=-1))
        if g % 2 == 1:
            send(high, high, e_s.at[g, 2], e_r.at[g, 2], dev(dy=-2))

    def back(g):
        arrived(D.at[g, yi(-1)], d_s.at[g, 2], d_r.at[g, 2])
        arrived(D.at[g, yi(1)], d_s.at[g, 3], d_r.at[g, 3])
        arrived(D.at[g, yi(-3)], e_s.at[g, 0], e_r.at[g, 0])
        arrived(D.at[g, yi(3)], e_s.at[g, 1], e_r.at[g, 1])
        arrived(D.at[g, yi(4)], e_s.at[g, 2], e_r.at[g, 2])
        pair = D[g].reshape(128, WIDE)
        total = jnp.dot(pair[:, PAD : 2 * PAD], WE[0], preferred_element_type=F32) + jnp.dot(
            pair[:, 2 * PAD :], WE[1], preferred_element_type=F32
        )
        total = total.reshape(2, 2, NX, 8, FEATS)
        for s in range(2):
            for k in range(2):
                GTS[g, k, s] = total[s, k]
        send(GTS.at[g, 1 - c], GR.at[g], g_s.at[g], g_r.at[g], dev(dc=1))

    def over_x(g):
        arrived(GR.at[g], g_s.at[g], g_r.at[g])

        def mine(k):
            return [GTS[g, c, s, xi(k)] + GR[g, s, xi(k)] for s in range(2)]

        for k in (2, 1, 3):
            XS[g, k - 1] = jnp.concatenate(mine(k), axis=0).astype(BF16)
            send(XS.at[g, k - 1], XR.at[g, k - 1], h_s.at[g, k - 1], h_r.at[g, k - 1], dev(dx=k))
        KX[g] = jnp.concatenate(mine(0), axis=0)

    def over_z(g):
        total = KX[g]
        for k in (1, 3, 2):
            arrived(XR.at[g, k - 1], h_s.at[g, k - 1], h_r.at[g, k - 1])
            total = total + XR[g, k - 1].astype(F32)
        for s, d in enumerate(GROUPS[g]):
            part = total[s * 8 : s * 8 + 8]
            if d == 0:
                ZO[...] = part
            else:
                i = d + 3
                ZS[i] = part
                send(ZS.at[i], ZR.at[i], k_s.at[i], k_r.at[i], dev(dz=d))

    def weights(i, out):
        other = (GRDS, TOKS, TOKS)[i]
        full = lax.dot_general(
            D[...].reshape(512, WIDE)[:, i * PAD : (i + 1) * PAD],
            other[...],
            (((0,), (0,)), ((), ())),
            preferred_element_type=F32,
        )
        out[...] = (full[:UNITS] * KEEP[(2, 0, 1)[i]].astype(F32)).astype(BF16)

    ring(1)
    partial(0)
    ring(2)
    partial(1)
    relay(0)
    ring(3)
    partial(2)
    relay(1)
    owned(0)
    ring(4)
    partial(3)
    relay(2)
    owned(1)
    spread(0)
    relay(3)
    owned(2)
    spread(1)
    back(0)
    owned(3)
    spread(2)
    back(1)
    over_x(0)
    spread(3)
    back(2)
    over_x(1)
    over_z(0)
    back(3)
    over_x(2)
    over_z(1)
    weights(0, o_d)
    over_x(3)
    over_z(2)
    weights(1, o_g)
    over_z(3)
    weights(2, o_u)
    total = ZO[...]
    for d in (1, -1, 2, -2, 3, -3, 4):
        arrived(ZR.at[d + 3], k_s.at[d + 3], k_r.at[d + 3])
        total = total + ZR[d + 3]
    o_t[...] = total.astype(BF16)
    for cp in sends:
        cp.wait_send()


def shards(tokens, out_grad, w_gate, w_up, w_down, mask_gate, mask_up, mask_down):
    vm = pltpu.VMEM
    dma = pltpu.SemaphoreType.DMA
    n = len(GROUPS)
    scratch = [
        vm((8, FEATS), BF16), vm((8, FEATS), BF16), vm((3, UNITS, FEATS), BF16),
        vm((3,) + mask_gate.shape, jnp.int32),
        vm((NZ, 2, NX, 16, FEATS), BF16), vm((3, PAD, FEATS), BF16), vm((3, UNITS, FEATS), BF16),
        vm((512, FEATS), BF16), vm((512, FEATS), BF16), vm((n, NY, 16, WIDE), F32),
        vm((n, 2, 16, WIDE), BF16), vm((n, 2, 16, WIDE), BF16), vm((n, 16, WIDE), BF16),
        vm((n, 2, 16, WIDE), BF16), vm((n, 2, 16, WIDE), BF16), vm((n, 16, WIDE), BF16),
        vm((n, 16, WIDE), BF16), vm((n, 16, WIDE), BF16), vm((n, 16, WIDE), BF16), vm((n, 16, WIDE), BF16),
        vm((n, NY, 16, WIDE), BF16),
        vm((n, 2, 2, NX, 8, FEATS), F32), vm((n, 2, NX, 8, FEATS), F32),
        vm((n, 3, 16, FEATS), BF16), vm((n, 3, 16, FEATS), BF16), vm((n, 16, FEATS), F32),
        vm((8, 8, FEATS), F32), vm((8, 8, FEATS), F32), vm((8, FEATS), F32),
        dma((8,)),
        dma((3,)), dma((3,)), dma((2, 4, 4)), dma((2, 4, 4)), dma((8,)), dma((8,)),
        dma((n, 3)), dma((n, 3)), dma((n, 2)), dma((n, 2)), dma((n, 4)), dma((n, 4)),
        dma((n, 3)), dma((n, 3)), dma((n,)), dma((n,)), dma((n, 3)), dma((n, 3)), dma((8,)), dma((8,)),
    ]
    outs = [jax.ShapeDtypeStruct(tokens.shape, BF16)] + [
        jax.ShapeDtypeStruct(w_gate.shape, BF16) for _ in range(3)
    ]
    return pl.pallas_call(
        kernel,
        out_shape=outs,
        in_specs=[pl.BlockSpec(memory_space=pl.ANY)] * 8,
        out_specs=[pl.BlockSpec(memory_space=pltpu.VMEM)] * 4,
        scratch_shapes=scratch,
        compiler_params=pltpu.CompilerParams(
            collective_id=0, has_side_effects=True, vmem_limit_bytes=40 * 1024 * 1024
        ),
        name="ffn_backward",
    )(tokens, out_grad, w_gate, w_up, w_down, mask_gate, mask_up, mask_down)


def solution(mesh):
    spec = P("row", "col")
    return jax.shard_map(
        shards,
        mesh=mesh,
        in_specs=(spec,) * 5 + (P(),) * 3,
        out_specs=(spec,) * 4,
        check_vma=False,
    )
```

```python
import jax
import jax.numpy as jnp
from jax import lax
from jax.experimental import pallas as pl
from jax.experimental.pallas import tpu as pltpu
from jax.sharding import PartitionSpec as P

NZ, NX, NY = 8, 4, 8
UNITS, FEATS, PAD = 224, 1024, 256
WIDE = 3 * PAD
TOKENS = 512
GROUPS = ((0,), (4,), (3,), (-3,), (2,), (-2,), (1,), (-1,))
N, S = len(GROUPS), len(GROUPS[0])
SLABS = tuple(o for g in GROUPS for o in g)
RO = 8 * S
F32, BF16 = jnp.float32, jnp.bfloat16
NN = (((1,), (0,)), ((), ()))
NT = (((1,), (1,)), ((), ()))
TN = (((0,), (0,)), ((), ()))


ORDER = (
    (2, 0), (2, 1), (2, 2), (1, 0), (0, 4), (3, 0), (0, 3), (0, -3), (0, 2), (0, -2),
    (0, 1), (0, -1), (1, 4), (4, 0), (3, 1), (1, 3), (1, -3), (5, 0), (3, 2), (1, 2),
    (3, 3), (4, 1), (1, -2), (3, 4), (6, 0), (1, 1), (4, 2), (3, 5), (4, 3), (1, -1),
    (3, 6), (5, 1), (4, 4), (3, 7), (7, 0), (5, 2), (4, 5), (5, 3), (8, 0), (4, 6),
    (6, 1), (5, 4), (4, 7), (6, 2), (9, 0), (5, 5), (6, 3), (5, 6), (7, 1), (6, 4),
    (5, 7), (7, 2), (8, 1), (6, 5), (7, 3), (6, 6), (8, 2), (7, 4), (6, 7), (8, 3),
    (10, 0), (9, 1), (7, 5), (8, 4), (7, 6), (9, 2), (8, 5), (9, 3), (7, 7), (8, 6),
    (12, 0), (9, 4), (8, 7), (11, 0), (9, 5), (9, 6), (9, 7), (13, 0),
)


def dot(a, b, dims):
    return lax.dot_general(a, b, dims, preferred_element_type=F32)


def expand(mask, row_start, col_start):
    wide, blocks = mask.shape
    unit = (row_start + lax.broadcasted_iota(jnp.int32, (UNITS, blocks), 0)) >> 7
    left = (unit == lax.broadcasted_iota(jnp.int32, (UNITS, blocks), 1)).astype(F32).astype(BF16)
    feat = (col_start + lax.broadcasted_iota(jnp.int32, (wide, FEATS), 1)) >> 7
    right = (feat == lax.broadcasted_iota(jnp.int32, (wide, FEATS), 0)).astype(F32).astype(BF16)
    inner = dot(left, mask.astype(F32).astype(BF16), NT)
    return dot(inner.astype(BF16), right, NN)


def kernel(
    tok, grd, wg, wu, wd, mg, mu, md,
    o_t, o_g, o_u, o_d,
    tokv, grdv, wv, mv, G, WE, WT, KEEP, TOKS, GRDS, P32,
    S1, R1, S3, R3, DG, DC, HID, GTS, GR, XS, XR, KX, ZS, ZR, ZO,
    lsem, out_sem, x_r, z_r, c_r, y1_r, y2_r, d_r, e_r, g_r, h_r, k_r, n_r,
):
    row, y = lax.axis_index("row"), lax.axis_index("col")
    c = lax.rem(row, 2)
    x = lax.rem(row // 2, NX)
    z = row // (2 * NX)

    def zi(d):
        return lax.rem(z + (d + NZ), NZ)

    def xi(d):
        return lax.rem(x + (d + NX), NX)

    def yi(d):
        return lax.rem(y + (d + NY), NY)

    def dev(dz=0, dx=0, dc=0, dy=0):
        return ((zi(dz) * NX + xi(dx)) * 2 + lax.rem(c + dc, 2), yi(dy))

    x_s, z_s, c_s, y1_s, y2_s, d_s, g_s, h_s, k_s, n_s = (out_sem.at[i] for i in range(10))

    def copy(src, dst, ssem, rsem, where):
        return pltpu.make_async_remote_copy(
            src, dst, ssem, rsem, device_id=where, device_id_type=pl.DeviceIdType.MESH
        )

    def send(src, dst, ssem, rsem, where):
        copy(src, dst, ssem, rsem, where).start()

    def arrived(ref, rsem):
        copy(ref, ref, out_sem.at[0], rsem, dev(dc=1)).wait_recv()

    def left(ref, ssem):
        copy(ref, ref, ssem, k_r.at[0], dev(dc=1)).wait_send()

    peers = (
        [dev(dc=1)]
        + [dev(dx=k) for k in (1, 2, 3)]
        + [dev(dz=k) for k in range(1, 8)]
        + [dev(dy=k) for k in range(1, 8)]
    )
    barrier = pltpu.get_barrier_semaphore()
    for p in peers:
        pl.semaphore_signal(barrier, inc=1, device_id=p, device_id_type=pl.DeviceIdType.MESH)
    loads = [
        pltpu.make_async_copy(s, d, lsem.at[i])
        for i, (s, d) in enumerate(
            (
                (tok, tokv), (grd, grdv),
                (mg, mv.at[0]), (mu, mv.at[1]), (md, mv.at[2]),
                (wg, wv.at[0]), (wu, wv.at[1]), (wd, wv.at[2]),
            )
        )
    ]
    for cp in loads:
        cp.start()
    loads[0].wait()
    loads[1].wait()
    G[z, c, x] = jnp.concatenate([tokv[...].astype(F32), grdv[...].astype(F32)], axis=0).astype(BF16)
    pl.semaphore_wait(barrier, len(peers))

    def over(o):
        ref = G.at[zi(o), c, x]
        for k in (1, 3, 2):
            send(ref, ref, x_s, x_r.at[o + 3], dev(dx=k))

    def fwd(o):
        i = (-o if o < 4 else 4) + 3
        arrived(G.at[zi(o), c, x], z_r.at[i])
        over(o)

    def slab(o):
        arrived(G.at[zi(o), c, 0:3], x_r.at[o + 3])
        ref = G.at[zi(o), c]
        send(ref, ref, c_s, c_r.at[o + 3], dev(dc=1))

    own = G.at[z, c, x]
    over(0)
    for d in (4, -3, 3, -2, 2, -1, 1):
        send(own, own, z_s, z_r.at[d + 3], dev(dz=d))

    def prep(i):
        loads[2 + i].wait()
        loads[5 + i].wait()
        keep = expand(mv[i], row * UNITS, y * FEATS)
        KEEP[i] = keep.astype(BF16)
        eff = jnp.concatenate(
            [(wv[i].astype(F32) * keep).astype(BF16), jnp.zeros((PAD - UNITS, FEATS), BF16)], axis=0
        )
        WE[i * PAD : (i + 1) * PAD] = eff
        WT[:, i * PAD : (i + 1) * PAD] = eff.T

    def partial(g):
        toks, grds = [], []
        for o in GROUPS[g]:
            arrived(G.at[zi(o), 1 - c], c_r.at[o + 3])
            v = G[zi(o)].astype(F32)
            toks.append(v[:, :, :8].reshape(64, FEATS))
            grds.append(v[:, :, 8:].reshape(64, FEATS))
        t = jnp.concatenate(toks, axis=0).astype(BF16)
        r = jnp.concatenate(grds, axis=0).astype(BF16)
        at = slice(g * 64 * S, (g + 1) * 64 * S)
        TOKS[at] = t
        GRDS[at] = r
        P32[g, :, :, : 2 * PAD] = dot(t, WT[:, : 2 * PAD], NN).reshape(NY, RO, 2 * PAD)
        P32[g, :, :, 2 * PAD :] = dot(r, WT[:, 2 * PAD :], NN).reshape(NY, RO, PAD)
        for i, k in enumerate((1, 3, -1, -3, 4)):
            S1[g, i] = P32[g, yi(k)].astype(BF16)
        send(S1.at[g, 0:2], R1.at[g, 0:2], y1_s, y1_r.at[g], dev(dy=1))
        send(S1.at[g, 2:4], R1.at[g, 2:4], y1_s, y1_r.at[g], dev(dy=-1))
        send(S1.at[g, 4], R1.at[g, 4], y1_s, y1_r.at[g], dev(dy=2 if g % 2 == 0 else -2))

    def relay(g):
        arrived(R1.at[g], y1_r.at[g])
        up = P32[g, yi(2)] + R1[g, 1].astype(F32)
        down = P32[g, yi(-2)] + R1[g, 3].astype(F32)
        far = R1[g, 4].astype(F32)
        if g % 2 == 0:
            up = up + far
        else:
            down = down + far
        S3[g, 0] = up.astype(BF16)
        send(S3.at[g, 0], R3.at[g, 0], y2_s, y2_r.at[g], dev(dy=2))
        S3[g, 1] = down.astype(BF16)
        send(S3.at[g, 1], R3.at[g, 1], y2_s, y2_r.at[g], dev(dy=-2))

    def owned(g):
        arrived(R3.at[g], y2_r.at[g])
        total = (
            P32[g, y]
            + (R1[g, 0].astype(F32) + R1[g, 2].astype(F32))
            + (R3[g, 0].astype(F32) + R3[g, 1].astype(F32))
        )
        gate, upper, dhid = total[:, :PAD], total[:, PAD : 2 * PAD], total[:, 2 * PAD :]
        sig = jax.nn.sigmoid(gate)
        act = gate * sig
        dgate = dhid * upper * sig * (1.0 + gate * (1.0 - sig))
        DG[g, y] = jnp.concatenate([dgate, dhid * act], axis=1).astype(BF16)
        ref = DG.at[g, y]
        send(ref, ref, d_s, d_r.at[g, 0], dev(dy=2))
        send(ref, ref, d_s, d_r.at[g, 1], dev(dy=-2))
        send(ref, ref, d_s, e_r.at[g], dev(dy=1))
        send(ref, ref, d_s, e_r.at[g], dev(dy=-1))
        HID[y, g] = (act * upper).astype(BF16)

    def hid(_):
        ref = HID.at[y]
        send(ref, ref, n_s, n_r.at[0], dev(dy=2))
        send(ref, ref, n_s, n_r.at[1], dev(dy=-2))
        send(ref, ref, n_s, n_r.at[2], dev(dy=1))
        send(ref, ref, n_s, n_r.at[2], dev(dy=-1))

    def hid_spread(_):
        low, high = HID.at[yi(-2)], HID.at[yi(2)]
        arrived(low, n_r.at[0])
        send(low, low, n_s, n_r.at[2], dev(dy=1))
        send(low, low, n_s, n_r.at[2], dev(dy=2))
        arrived(high, n_r.at[1])
        send(high, high, n_s, n_r.at[2], dev(dy=-1))

    def spread(g):
        low, high = DG.at[g, yi(-2)], DG.at[g, yi(2)]
        arrived(low, d_r.at[g, 0])
        send(low, low, d_s, e_r.at[g], dev(dy=1))
        if g % 2 == 0:
            send(low, low, d_s, e_r.at[g], dev(dy=2))
        arrived(high, d_r.at[g, 1])
        send(high, high, d_s, e_r.at[g], dev(dy=-1))
        if g % 2 == 1:
            send(high, high, d_s, e_r.at[g], dev(dy=-2))

    def back(g):
        arrived(DG.at[g, 0:5], e_r.at[g])
        pair = DG[g].astype(F32).reshape(64 * S, 2 * PAD).astype(BF16)
        DC[g * 64 * S : (g + 1) * 64 * S] = pair
        total = dot(pair, WE[: 2 * PAD], NN).reshape(S, 2, NX, 8, FEATS)
        for s in range(S):
            for k in range(2):
                GTS[g, k, s] = total[s, k]
        send(GTS.at[g, 1 - c], GR.at[g], g_s, g_r.at[g], dev(dc=1))

    def over_x(g):
        arrived(GR.at[g], g_r.at[g])

        def mine(k):
            return jnp.concatenate([GTS[g, c, s, xi(k)] + GR[g, s, xi(k)] for s in range(S)], axis=0)

        for k in (2, 1, 3):
            XS[g, k - 1] = mine(k).astype(BF16)
            send(XS.at[g, k - 1], XR.at[g, k - 1], h_s, h_r.at[g], dev(dx=k))
        KX[g] = mine(0)

    def over_z(g):
        arrived(XR.at[g], h_r.at[g])
        total = KX[g] + XR[g, 0].astype(F32) + XR[g, 1].astype(F32) + XR[g, 2].astype(F32)
        for s, d in enumerate(GROUPS[g]):
            part = total[s * 8 : s * 8 + 8]
            if d == 0:
                ZO[...] = part
            else:
                i = d + 3
                ZS[i] = part
                send(ZS.at[i], ZR.at[i], k_s, k_r.at[0], dev(dz=d))

    def weights(i, left, right, out):
        out[...] = (dot(left, right[...], TN)[:UNITS] * KEEP[i].astype(F32)).astype(BF16)

    def pair_weights(_):
        weights(0, DC[:, :PAD], TOKS, o_g)
        weights(1, DC[:, PAD:], TOKS, o_u)

    def down_weights(_):
        arrived(HID.at[0:5], n_r.at[2])
        hidden = jnp.concatenate(
            [HID[:, g].astype(F32).reshape(64 * S, PAD) for g in range(N)], axis=0
        ).astype(BF16)
        weights(2, hidden, GRDS, o_d)

    stages = (
        fwd, slab, prep, partial, relay, owned, spread, back, over_x, over_z,
        hid, hid_spread, pair_weights, down_weights,
    )
    for stage, at in ORDER:
        stages[stage](at)
    arrived(ZR.at[0:7], k_r.at[0])
    total = ZO[...]
    for d in (1, -1, 2, -2, 3, -3, 4):
        total = total + ZR[d + 3]
    o_t[...] = total.astype(BF16)
    for ref, ssem in (
        (G.at[0:3], x_s), (G.at[0:7, 0, 0], z_s), (G.at[:, 0], c_s), (S1, y1_s), (S3, y2_s),
        (DG.at[:, 0:7], d_s), (GTS.at[:, 0], g_s), (XS, h_s), (ZS.at[0:7], k_s), (HID.at[0:7], n_s),
    ):
        left(ref, ssem)


def store(a, b, c, d, oa, ob, oc, od, sem):
    copies = [
        pltpu.make_async_copy(s, t, sem.at[i])
        for i, (s, t) in enumerate(((a, oa), (b, ob), (c, oc), (d, od)))
    ]
    for cp in copies:
        cp.start()
    for cp in copies:
        cp.wait()


def shards(tokens, out_grad, w_gate, w_up, w_down, mask_gate, mask_up, mask_down):
    vm = pltpu.VMEM
    dma = pltpu.SemaphoreType.DMA
    scratch = [
        vm((8, FEATS), BF16), vm((8, FEATS), BF16), vm((3, UNITS, FEATS), BF16),
        vm((3,) + mask_gate.shape[::-1], jnp.int32),
        vm((NZ, 2, NX, 16, FEATS), BF16), vm((WIDE, FEATS), BF16), vm((FEATS, WIDE), BF16),
        vm((3, UNITS, FEATS), BF16),
        vm((TOKENS, FEATS), BF16), vm((TOKENS, FEATS), BF16), vm((N, NY, RO, WIDE), F32),
        vm((N, 5, RO, WIDE), BF16), vm((N, 5, RO, WIDE), BF16), vm((N, 2, RO, WIDE), BF16), vm((N, 2, RO, WIDE), BF16),
        vm((N, NY, RO, 2 * PAD), BF16), vm((TOKENS, 2 * PAD), BF16), vm((NY, N, RO, PAD), BF16),
        vm((N, 2, S, NX, 8, FEATS), F32), vm((N, S, NX, 8, FEATS), F32),
        vm((N, 3, RO, FEATS), BF16), vm((N, 3, RO, FEATS), BF16), vm((N, RO, FEATS), F32),
        vm((8, 8, FEATS), F32), vm((8, 8, FEATS), F32), vm((8, FEATS), F32),
        dma((8,)),
        dma((10,)), dma((8,)), dma((8,)), dma((8,)), dma((N,)), dma((N,)), dma((N, 2)), dma((N,)),
        dma((N,)), dma((N,)), dma((1,)), dma((3,)),
    ]
    outs = [jax.ShapeDtypeStruct(tokens.shape, BF16)] + [
        jax.ShapeDtypeStruct(w_gate.shape, BF16) for _ in range(3)
    ]
    operands = [
        pltpu.with_memory_space_constraint(a, pltpu.HBM)
        for a in (tokens, out_grad, w_gate, w_up, w_down, mask_gate.T, mask_up.T, mask_down.T)
    ]
    results = pl.pallas_call(
        kernel,
        out_shape=outs,
        in_specs=[pl.BlockSpec(memory_space=pltpu.HBM)] * 8,
        out_specs=[pl.BlockSpec(memory_space=pltpu.VMEM)] * 4,
        scratch_shapes=scratch,
        compiler_params=pltpu.CompilerParams(
            collective_id=0, has_side_effects=True, vmem_limit_bytes=40 * 1024 * 1024
        ),
        name="ffn_backward",
    )(*operands)
    return pl.pallas_call(
        store,
        out_shape=outs,
        in_specs=[pl.BlockSpec(memory_space=pltpu.VMEM)] * 4,
        out_specs=[pl.BlockSpec(memory_space=pltpu.HBM)] * 4,
        scratch_shapes=[dma((4,))],
        compiler_params=pltpu.CompilerParams(vmem_limit_bytes=8 * 1024 * 1024),
        name="store_results",
    )(*results)


def solution(mesh):
    spec = P("row", "col")
    return jax.shard_map(
        shards,
        mesh=mesh,
        in_specs=(spec,) * 5 + (P(),) * 3,
        out_specs=(spec,) * 4,
        check_vma=False,
    )
```

```python
import jax
import jax.numpy as jnp
from jax import lax
from jax.experimental import pallas as pl
from jax.experimental.pallas import tpu as pltpu
from jax.sharding import PartitionSpec as P

NZ, NX, NY = 8, 4, 8
UNITS, FEATS, PAD = 224, 1024, 256
WIDE = 3 * PAD
TOKENS = 512
GROUPS = ((0,), (4,), (1,), (-1,), (3,), (-3,), (2,), (-2,))
N, S = len(GROUPS), len(GROUPS[0])
SLABS = tuple(o for g in GROUPS for o in g)
RO = 8 * S
F32, BF16 = jnp.float32, jnp.bfloat16
NN = (((1,), (0,)), ((), ()))
NT = (((1,), (1,)), ((), ()))
TN = (((0,), (0,)), ((), ()))


ORDER = (
    (2, 0), (2, 1), (2, 2), (1, 0), (0, 4), (3, 0), (0, 3), (0, -3), (0, 2), (0, -2),
    (1, 4), (4, 0), (1, 1), (1, -1), (3, 1), (1, 3), (3, 2), (3, 3), (1, -3), (3, 4),
    (5, 0), (1, 2), (3, 5), (4, 1), (1, -2), (3, 6), (4, 2), (4, 3), (3, 7), (4, 4),
    (6, 0), (4, 5), (5, 1), (4, 6), (5, 2), (5, 3), (4, 7), (5, 4), (7, 0), (5, 5),
    (6, 1), (5, 6), (6, 2), (8, 0), (6, 3), (5, 7), (6, 4), (6, 5), (7, 1), (6, 6),
    (9, 0), (7, 2), (7, 3), (6, 7), (8, 1), (7, 4), (8, 2), (7, 5), (8, 3), (7, 6),
    (8, 4), (10, 0), (8, 5), (9, 1), (7, 7), (8, 6), (9, 2), (12, 0), (8, 7), (9, 3),
    (9, 4), (9, 5), (11, 0), (9, 6), (9, 7), (13, 0),
)


def dot(a, b, dims):
    return lax.dot_general(a, b, dims, preferred_element_type=F32)


def expand(mask, row_start, col_start):
    wide, blocks = mask.shape
    unit = (row_start + lax.broadcasted_iota(jnp.int32, (UNITS, blocks), 0)) >> 7
    left = (unit == lax.broadcasted_iota(jnp.int32, (UNITS, blocks), 1)).astype(F32).astype(BF16)
    feat = (col_start + lax.broadcasted_iota(jnp.int32, (wide, FEATS), 1)) >> 7
    right = (feat == lax.broadcasted_iota(jnp.int32, (wide, FEATS), 0)).astype(F32).astype(BF16)
    inner = dot(left, mask.astype(F32).astype(BF16), NT)
    return dot(inner.astype(BF16), right, NN)


def kernel(
    tok, grd, wg, wu, wd, mg, mu, md,
    o_t, o_g, o_u, o_d,
    tokv, grdv, wv, mv, G, WE, WT, KEEP, TOKS, GRDS, P32,
    S1, R1, S3, R3, DG, DC, HID, GTS, GR, XS, XR, KX, ZS, ZR, ZO,
    lsem, out_sem, x_r, z_r, c_r, y1_r, y2_r, d_r, e_r, g_r, h_r, k_r, n_r,
):
    row, y = lax.axis_index("row"), lax.axis_index("col")
    c = lax.rem(row, 2)
    x = lax.rem(row // 2, NX)
    z = row // (2 * NX)

    def zi(d):
        return lax.rem(z + (d + NZ), NZ)

    def xi(d):
        return lax.rem(x + (d + NX), NX)

    def yi(d):
        return lax.rem(y + (d + NY), NY)

    def dev(dz=0, dx=0, dc=0, dy=0):
        return ((zi(dz) * NX + xi(dx)) * 2 + lax.rem(c + dc, 2), yi(dy))

    x_s, z_s, c_s, y1_s, y2_s, d_s, g_s, h_s, k_s, n_s = (out_sem.at[i] for i in range(10))

    def copy(src, dst, ssem, rsem, where):
        return pltpu.make_async_remote_copy(
            src, dst, ssem, rsem, device_id=where, device_id_type=pl.DeviceIdType.MESH
        )

    def send(src, dst, ssem, rsem, where):
        copy(src, dst, ssem, rsem, where).start()

    def arrived(ref, rsem):
        copy(ref, ref, out_sem.at[0], rsem, dev(dc=1)).wait_recv()

    def left(ref, ssem):
        copy(ref, ref, ssem, k_r.at[0], dev(dc=1)).wait_send()

    peers = (
        [dev(dc=1)]
        + [dev(dx=k) for k in (1, 2, 3)]
        + [dev(dz=k) for k in range(1, 8)]
        + [dev(dy=k) for k in (1, 2, -1, -2)]
    )
    barrier = pltpu.get_barrier_semaphore()
    for p in peers:
        pl.semaphore_signal(barrier, inc=1, device_id=p, device_id_type=pl.DeviceIdType.MESH)
    loads = [
        pltpu.make_async_copy(s, d, lsem.at[i])
        for i, (s, d) in enumerate(
            (
                (tok, tokv), (grd, grdv),
                (mg, mv.at[0]), (mu, mv.at[1]), (md, mv.at[2]),
                (wg, wv.at[0]), (wu, wv.at[1]), (wd, wv.at[2]),
            )
        )
    ]
    for cp in loads:
        cp.start()
    loads[0].wait()
    loads[1].wait()
    G[z, c, x] = jnp.concatenate([tokv[...].astype(F32), grdv[...].astype(F32)], axis=0).astype(BF16)
    pl.semaphore_wait(barrier, len(peers))

    def over(o):
        ref = G.at[zi(o), c, x]
        for k in (1, 3, 2):
            send(ref, ref, x_s, x_r.at[o + 3], dev(dx=k))

    def fwd(o):
        i = (-o if o < 4 else 4) + 3
        arrived(G.at[zi(o), c, x], z_r.at[i])
        over(o)

    def slab(o):
        ref = G.at[zi(o), c]
        if abs(o) == 1:
            arrived(ref, z_r.at[3 - o])
        else:
            arrived(G.at[zi(o), c, 0:3], x_r.at[o + 3])
        send(ref, ref, c_s, c_r.at[o + 3], dev(dc=1))
        if o == 0:
            for d in (1, -1):
                send(ref, ref, c_s, z_r.at[d + 3], dev(dz=d))

    own = G.at[z, c, x]
    over(0)
    for d in (4, -3, 3, -2, 2):
        send(own, own, z_s, z_r.at[d + 3], dev(dz=d))

    def prep(i):
        loads[2 + i].wait()
        loads[5 + i].wait()
        keep = expand(mv[i], row * UNITS, y * FEATS)
        KEEP[i] = keep.astype(BF16)
        eff = jnp.concatenate(
            [(wv[i].astype(F32) * keep).astype(BF16), jnp.zeros((PAD - UNITS, FEATS), BF16)], axis=0
        )
        WE[i * PAD : (i + 1) * PAD] = eff
        WT[:, i * PAD : (i + 1) * PAD] = eff.T

    def partial(g):
        toks, grds = [], []
        for o in GROUPS[g]:
            arrived(G.at[zi(o), 1 - c], c_r.at[o + 3])
            v = G[zi(o)].astype(F32)
            toks.append(v[:, :, :8].reshape(64, FEATS))
            grds.append(v[:, :, 8:].reshape(64, FEATS))
        t = jnp.concatenate(toks, axis=0).astype(BF16)
        r = jnp.concatenate(grds, axis=0).astype(BF16)
        at = slice(g * 64 * S, (g + 1) * 64 * S)
        TOKS[at] = t
        GRDS[at] = r
        P32[g, :, :, : 2 * PAD] = dot(t, WT[:, : 2 * PAD], NN).reshape(NY, RO, 2 * PAD)
        P32[g, :, :, 2 * PAD :] = dot(r, WT[:, 2 * PAD :], NN).reshape(NY, RO, PAD)
        for i, k in enumerate((1, 3, -1, -3, 4)):
            S1[g, i] = P32[g, yi(k)].astype(BF16)
        send(S1.at[g, 0:2], R1.at[g, 0:2], y1_s, y1_r.at[g], dev(dy=1))
        send(S1.at[g, 2:4], R1.at[g, 2:4], y1_s, y1_r.at[g], dev(dy=-1))
        send(S1.at[g, 4], R1.at[g, 4], y1_s, y1_r.at[g], dev(dy=2 if g % 2 == 0 else -2))

    def relay(g):
        arrived(R1.at[g], y1_r.at[g])
        up = P32[g, yi(2)] + R1[g, 1].astype(F32)
        down = P32[g, yi(-2)] + R1[g, 3].astype(F32)
        far = R1[g, 4].astype(F32)
        if g % 2 == 0:
            up = up + far
        else:
            down = down + far
        S3[g, 0] = up.astype(BF16)
        send(S3.at[g, 0], R3.at[g, 0], y2_s, y2_r.at[g], dev(dy=2))
        S3[g, 1] = down.astype(BF16)
        send(S3.at[g, 1], R3.at[g, 1], y2_s, y2_r.at[g], dev(dy=-2))

    def owned(g):
        arrived(R3.at[g], y2_r.at[g])
        total = (
            P32[g, y]
            + (R1[g, 0].astype(F32) + R1[g, 2].astype(F32))
            + (R3[g, 0].astype(F32) + R3[g, 1].astype(F32))
        )
        gate, upper, dhid = total[:, :PAD], total[:, PAD : 2 * PAD], total[:, 2 * PAD :]
        sig = jax.nn.sigmoid(gate)
        act = gate * sig
        dgate = dhid * upper * sig * (1.0 + gate * (1.0 - sig))
        DG[g, y] = jnp.concatenate([dgate, dhid * act], axis=1).astype(BF16)
        ref = DG.at[g, y]
        send(ref, ref, d_s, d_r.at[g, 0], dev(dy=2))
        send(ref, ref, d_s, d_r.at[g, 1], dev(dy=-2))
        send(ref, ref, d_s, e_r.at[g], dev(dy=1))
        send(ref, ref, d_s, e_r.at[g], dev(dy=-1))
        HID[y, g] = (act * upper).astype(BF16)

    def hid(_):
        ref = HID.at[y]
        send(ref, ref, n_s, n_r.at[0], dev(dy=2))
        send(ref, ref, n_s, n_r.at[1], dev(dy=-2))
        send(ref, ref, n_s, n_r.at[2], dev(dy=1))
        send(ref, ref, n_s, n_r.at[2], dev(dy=-1))

    def hid_spread(_):
        low, high = HID.at[yi(-2)], HID.at[yi(2)]
        arrived(low, n_r.at[0])
        send(low, low, n_s, n_r.at[2], dev(dy=1))
        send(low, low, n_s, n_r.at[2], dev(dy=2))
        arrived(high, n_r.at[1])
        send(high, high, n_s, n_r.at[2], dev(dy=-1))

    def spread(g):
        low, high = DG.at[g, yi(-2)], DG.at[g, yi(2)]
        arrived(low, d_r.at[g, 0])
        send(low, low, d_s, e_r.at[g], dev(dy=1))
        if g % 2 == 0:
            send(low, low, d_s, e_r.at[g], dev(dy=2))
        arrived(high, d_r.at[g, 1])
        send(high, high, d_s, e_r.at[g], dev(dy=-1))
        if g % 2 == 1:
            send(high, high, d_s, e_r.at[g], dev(dy=-2))

    def back(g):
        arrived(DG.at[g, 0:5], e_r.at[g])
        pair = DG[g].astype(F32).reshape(64 * S, 2 * PAD).astype(BF16)
        DC[g * 64 * S : (g + 1) * 64 * S] = pair
        total = dot(pair, WE[: 2 * PAD], NN).reshape(S, 2, NX, 8, FEATS)
        for s in range(S):
            for k in range(2):
                GTS[g, k, s] = total[s, k]
        send(GTS.at[g, 1 - c], GR.at[g], g_s, g_r.at[g], dev(dc=1))

    def over_x(g):
        arrived(GR.at[g], g_r.at[g])

        def mine(k):
            return jnp.concatenate([GTS[g, c, s, xi(k)] + GR[g, s, xi(k)] for s in range(S)], axis=0)

        for k in (2, 1, 3):
            XS[g, k - 1] = mine(k).astype(BF16)
            send(XS.at[g, k - 1], XR.at[g, k - 1], h_s, h_r.at[g], dev(dx=k))
        KX[g] = mine(0)

    def over_z(g):
        arrived(XR.at[g], h_r.at[g])
        total = KX[g] + XR[g, 0].astype(F32) + XR[g, 1].astype(F32) + XR[g, 2].astype(F32)
        for s, d in enumerate(GROUPS[g]):
            part = total[s * 8 : s * 8 + 8]
            if d == 0:
                ZO[...] = part
            else:
                i = d + 3
                ZS[i] = part
                send(ZS.at[i], ZR.at[i], k_s, k_r.at[0], dev(dz=d))

    def weights(i, left, right, out):
        out[...] = (dot(left, right[...], TN)[:UNITS] * KEEP[i].astype(F32)).astype(BF16)

    def pair_weights(_):
        weights(0, DC[:, :PAD], TOKS, o_g)
        weights(1, DC[:, PAD:], TOKS, o_u)

    def down_weights(_):
        arrived(HID.at[0:5], n_r.at[2])
        hidden = jnp.concatenate(
            [HID[:, g].astype(F32).reshape(64 * S, PAD) for g in range(N)], axis=0
        ).astype(BF16)
        weights(2, hidden, GRDS, o_d)

    stages = (
        fwd, slab, prep, partial, relay, owned, spread, back, over_x, over_z,
        hid, hid_spread, pair_weights, down_weights,
    )
    for stage, at in ORDER:
        stages[stage](at)
    arrived(ZR.at[0:7], k_r.at[0])
    total = ZO[...]
    for d in (1, -1, 2, -2, 3, -3, 4):
        total = total + ZR[d + 3]
    o_t[...] = total.astype(BF16)
    for ref, ssem in (
        (G.at[0:3, :, 0:3], x_s), (G.at[0:5, 0, 0], z_s), (G.at[0:5], c_s), (S1, y1_s), (S3, y2_s),
        (DG.at[:, 0:7], d_s), (GTS.at[:, 0], g_s), (XS, h_s), (ZS.at[0:7], k_s), (HID.at[0:7], n_s),
    ):
        left(ref, ssem)


def store(a, b, c, d, oa, ob, oc, od, sem):
    copies = [
        pltpu.make_async_copy(s, t, sem.at[i])
        for i, (s, t) in enumerate(((a, oa), (b, ob), (c, oc), (d, od)))
    ]
    for cp in copies:
        cp.start()
    for cp in copies:
        cp.wait()


def shards(tokens, out_grad, w_gate, w_up, w_down, mask_gate, mask_up, mask_down):
    vm = pltpu.VMEM
    dma = pltpu.SemaphoreType.DMA
    scratch = [
        vm((8, FEATS), BF16), vm((8, FEATS), BF16), vm((3, UNITS, FEATS), BF16),
        vm((3,) + mask_gate.shape[::-1], jnp.int32),
        vm((NZ, 2, NX, 16, FEATS), BF16), vm((WIDE, FEATS), BF16), vm((FEATS, WIDE), BF16),
        vm((3, UNITS, FEATS), BF16),
        vm((TOKENS, FEATS), BF16), vm((TOKENS, FEATS), BF16), vm((N, NY, RO, WIDE), F32),
        vm((N, 5, RO, WIDE), BF16), vm((N, 5, RO, WIDE), BF16), vm((N, 2, RO, WIDE), BF16), vm((N, 2, RO, WIDE), BF16),
        vm((N, NY, RO, 2 * PAD), BF16), vm((TOKENS, 2 * PAD), BF16), vm((NY, N, RO, PAD), BF16),
        vm((N, 2, S, NX, 8, FEATS), F32), vm((N, S, NX, 8, FEATS), F32),
        vm((N, 3, RO, FEATS), BF16), vm((N, 3, RO, FEATS), BF16), vm((N, RO, FEATS), F32),
        vm((8, 8, FEATS), F32), vm((8, 8, FEATS), F32), vm((8, FEATS), F32),
        dma((8,)),
        dma((10,)), dma((8,)), dma((8,)), dma((8,)), dma((N,)), dma((N,)), dma((N, 2)), dma((N,)),
        dma((N,)), dma((N,)), dma((1,)), dma((3,)),
    ]
    outs = [jax.ShapeDtypeStruct(tokens.shape, BF16)] + [
        jax.ShapeDtypeStruct(w_gate.shape, BF16) for _ in range(3)
    ]
    operands = [
        pltpu.with_memory_space_constraint(a, pltpu.HBM)
        for a in (tokens, out_grad, w_gate, w_up, w_down, mask_gate.T, mask_up.T, mask_down.T)
    ]
    results = pl.pallas_call(
        kernel,
        out_shape=outs,
        in_specs=[pl.BlockSpec(memory_space=pltpu.HBM)] * 8,
        out_specs=[pl.BlockSpec(memory_space=pltpu.VMEM)] * 4,
        scratch_shapes=scratch,
        compiler_params=pltpu.CompilerParams(
            collective_id=0, has_side_effects=True, vmem_limit_bytes=40 * 1024 * 1024
        ),
        name="ffn_backward",
    )(*operands)
    return pl.pallas_call(
        store,
        out_shape=outs,
        in_specs=[pl.BlockSpec(memory_space=pltpu.VMEM)] * 4,
        out_specs=[pl.BlockSpec(memory_space=pltpu.HBM)] * 4,
        scratch_shapes=[dma((4,))],
        compiler_params=pltpu.CompilerParams(vmem_limit_bytes=8 * 1024 * 1024),
        name="store_results",
    )(*results)


def solution(mesh):
    spec = P("row", "col")
    return jax.shard_map(
        shards,
        mesh=mesh,
        in_specs=(spec,) * 5 + (P(),) * 3,
        out_specs=(spec,) * 4,
        check_vma=False,
    )
```

```python
import jax
import jax.numpy as jnp
from jax import lax
from jax.experimental import pallas as pl
from jax.experimental.pallas import tpu as pltpu
from jax.sharding import PartitionSpec as P

NZ, NX, NY = 8, 4, 8
UNITS, FEATS, PAD = 224, 1024, 256
WIDE = 3 * PAD
TOKENS = 512
GROUPS = ((0,), (4,), (1,), (-1,), (3,), (-3,), (2,), (-2,))
N, S = len(GROUPS), len(GROUPS[0])
SLABS = tuple(o for g in GROUPS for o in g)
RO = 8 * S
F32, BF16 = jnp.float32, jnp.bfloat16
NN = (((1,), (0,)), ((), ()))
NT = (((1,), (1,)), ((), ()))
TN = (((0,), (0,)), ((), ()))


ORDER = (
    (2, 0), (2, 1), (2, 2), (1, 0), (0, 4), (3, 0), (0, 3), (0, -3), (0, 2), (0, -2),
    (1, 4), (4, 0), (1, 1), (1, -1), (3, 1), (1, 3), (3, 2), (3, 3), (1, -3), (3, 4),
    (5, 0), (1, 2), (3, 5), (4, 1), (1, -2), (3, 6), (4, 2), (4, 3), (3, 7), (4, 4),
    (6, 0), (4, 5), (5, 1), (4, 6), (5, 2), (5, 3), (4, 7), (5, 4), (7, 0), (5, 5),
    (6, 1), (5, 6), (6, 2), (8, 0), (6, 3), (5, 7), (6, 4), (6, 5), (7, 1), (6, 6),
    (9, 0), (7, 2), (7, 3), (6, 7), (8, 1), (7, 4), (8, 2), (7, 5), (8, 3), (7, 6),
    (8, 4), (10, 0), (8, 5), (9, 1), (7, 7), (8, 6), (9, 2), (12, 0), (8, 7), (9, 3),
    (9, 4), (9, 5), (11, 0), (9, 6), (9, 7), (13, 0),
)


def dot(a, b, dims):
    return lax.dot_general(a, b, dims, preferred_element_type=F32)


def expand(mask, row_start, col_start):
    wide, blocks = mask.shape
    unit = (row_start + lax.broadcasted_iota(jnp.int32, (UNITS, blocks), 0)) >> 7
    left = (unit == lax.broadcasted_iota(jnp.int32, (UNITS, blocks), 1)).astype(F32).astype(BF16)
    feat = (col_start + lax.broadcasted_iota(jnp.int32, (wide, FEATS), 1)) >> 7
    right = (feat == lax.broadcasted_iota(jnp.int32, (wide, FEATS), 0)).astype(F32).astype(BF16)
    inner = dot(left, mask.astype(F32).astype(BF16), NT)
    return dot(inner.astype(BF16), right, NN)


def kernel(
    tok, grd, wg, wu, wd, mg, mu, md,
    o_t, o_g, o_u, o_d,
    tokv, grdv, wv, mv, G, WE, WT, KEEP, TOKS, GRDS, P32,
    S1, R1, S3, R3, DG, DC, HID, GTS, GR, XS, XR, KX, ZS, ZR, ZO,
    lsem, out_sem, x_r, z_r, c_r, y1_r, y2_r, d_r, e_r, g_r, h_r, k_r, n_r,
):
    row, y = lax.axis_index("row"), lax.axis_index("col")
    c = lax.rem(row, 2)
    x = lax.rem(row // 2, NX)
    z = row // (2 * NX)

    def zi(d):
        return lax.rem(z + (d + NZ), NZ)

    def xi(d):
        return lax.rem(x + (d + NX), NX)

    def yi(d):
        return lax.rem(y + (d + NY), NY)

    def dev(dz=0, dx=0, dc=0, dy=0):
        return ((zi(dz) * NX + xi(dx)) * 2 + lax.rem(c + dc, 2), yi(dy))

    x_s, z_s, c_s, y1_s, y2_s, d_s, g_s, h_s, k_s, n_s = (out_sem.at[i] for i in range(10))

    def copy(src, dst, ssem, rsem, where):
        return pltpu.make_async_remote_copy(
            src, dst, ssem, rsem, device_id=where, device_id_type=pl.DeviceIdType.MESH
        )

    def send(src, dst, ssem, rsem, where):
        copy(src, dst, ssem, rsem, where).start()

    def arrived(ref, rsem):
        copy(ref, ref, out_sem.at[0], rsem, dev(dc=1)).wait_recv()

    def left(ref, ssem):
        copy(ref, ref, ssem, k_r.at[0], dev(dc=1)).wait_send()

    loads = [
        pltpu.make_async_copy(s, d, lsem.at[i])
        for i, (s, d) in enumerate(
            (
                (tok, tokv), (grd, grdv),
                (mg, mv.at[0]), (mu, mv.at[1]), (md, mv.at[2]),
                (wg, wv.at[0]), (wu, wv.at[1]), (wd, wv.at[2]),
            )
        )
    ]
    loads[0].start()
    loads[1].start()
    peers = (
        [dev(dz=k) for k in (4, 3, -3, 2, -2, 1, -1)]
        + [dev(dx=k) for k in (2, 1, 3)]
        + [dev(dy=k) for k in (2, -2, 1, -1)]
        + [dev(dc=1)]
    )
    barrier = pltpu.get_barrier_semaphore()
    for p in peers:
        pl.semaphore_signal(barrier, inc=1, device_id=p, device_id_type=pl.DeviceIdType.MESH)
    for cp in loads[2:]:
        cp.start()
    loads[0].wait()
    loads[1].wait()
    G[z, c, x] = jnp.concatenate([tokv[...].astype(F32), grdv[...].astype(F32)], axis=0).astype(BF16)
    pl.semaphore_wait(barrier, len(peers))

    def over(o):
        ref = G.at[zi(o), c, x]
        for k in (1, 3, 2):
            send(ref, ref, x_s, x_r.at[o + 3], dev(dx=k))

    def fwd(o):
        i = (-o if o < 4 else 4) + 3
        arrived(G.at[zi(o), c, x], z_r.at[i])
        over(o)

    def slab(o):
        ref = G.at[zi(o), c]
        if abs(o) == 1:
            arrived(ref, z_r.at[3 - o])
        else:
            arrived(G.at[zi(o), c, 0:3], x_r.at[o + 3])
        send(ref, ref, c_s, c_r.at[o + 3], dev(dc=1))
        if o == 0:
            for d in (1, -1):
                send(ref, ref, c_s, z_r.at[d + 3], dev(dz=d))

    own = G.at[z, c, x]
    over(0)
    for d in (4, -3, 3, -2, 2):
        send(own, own, z_s, z_r.at[d + 3], dev(dz=d))

    def prep(i):
        loads[2 + i].wait()
        loads[5 + i].wait()
        keep = expand(mv[i], row * UNITS, y * FEATS)
        KEEP[i] = keep.astype(BF16)
        eff = jnp.concatenate(
            [(wv[i].astype(F32) * keep).astype(BF16), jnp.zeros((PAD - UNITS, FEATS), BF16)], axis=0
        )
        WE[i * PAD : (i + 1) * PAD] = eff
        WT[:, i * PAD : (i + 1) * PAD] = eff.T

    def partial(g):
        toks, grds = [], []
        for o in GROUPS[g]:
            arrived(G.at[zi(o), 1 - c], c_r.at[o + 3])
            v = G[zi(o)].astype(F32)
            toks.append(v[:, :, :8].reshape(64, FEATS))
            grds.append(v[:, :, 8:].reshape(64, FEATS))
        t = jnp.concatenate(toks, axis=0).astype(BF16)
        r = jnp.concatenate(grds, axis=0).astype(BF16)
        at = slice(g * 64 * S, (g + 1) * 64 * S)
        TOKS[at] = t
        GRDS[at] = r
        P32[g, :, :, : 2 * PAD] = dot(t, WT[:, : 2 * PAD], NN).reshape(NY, RO, 2 * PAD)
        P32[g, :, :, 2 * PAD :] = dot(r, WT[:, 2 * PAD :], NN).reshape(NY, RO, PAD)
        for i, k in enumerate((1, 3, -1, -3, 4)):
            S1[g, i] = P32[g, yi(k)].astype(BF16)
        send(S1.at[g, 0:2], R1.at[g, 0:2], y1_s, y1_r.at[g], dev(dy=1))
        send(S1.at[g, 2:4], R1.at[g, 2:4], y1_s, y1_r.at[g], dev(dy=-1))
        send(S1.at[g, 4], R1.at[g, 4], y1_s, y1_r.at[g], dev(dy=2 if g % 2 == 0 else -2))

    def relay(g):
        arrived(R1.at[g], y1_r.at[g])
        up = P32[g, yi(2)] + R1[g, 1].astype(F32)
        down = P32[g, yi(-2)] + R1[g, 3].astype(F32)
        far = R1[g, 4].astype(F32)
        if g % 2 == 0:
            up = up + far
        else:
            down = down + far
        S3[g, 0] = up.astype(BF16)
        send(S3.at[g, 0], R3.at[g, 0], y2_s, y2_r.at[g], dev(dy=2))
        S3[g, 1] = down.astype(BF16)
        send(S3.at[g, 1], R3.at[g, 1], y2_s, y2_r.at[g], dev(dy=-2))

    def owned(g):
        arrived(R3.at[g], y2_r.at[g])
        total = (
            P32[g, y]
            + (R1[g, 0].astype(F32) + R1[g, 2].astype(F32))
            + (R3[g, 0].astype(F32) + R3[g, 1].astype(F32))
        )
        gate, upper, dhid = total[:, :PAD], total[:, PAD : 2 * PAD], total[:, 2 * PAD :]
        sig = jax.nn.sigmoid(gate)
        act = gate * sig
        dgate = dhid * upper * sig * (1.0 + gate * (1.0 - sig))
        DG[g, y] = jnp.concatenate([dgate, dhid * act], axis=1).astype(BF16)
        ref = DG.at[g, y]
        send(ref, ref, d_s, d_r.at[g, 0], dev(dy=2))
        send(ref, ref, d_s, d_r.at[g, 1], dev(dy=-2))
        send(ref, ref, d_s, e_r.at[g], dev(dy=1))
        send(ref, ref, d_s, e_r.at[g], dev(dy=-1))
        HID[y, g] = (act * upper).astype(BF16)

    def hid(_):
        ref = HID.at[y]
        send(ref, ref, n_s, n_r.at[0], dev(dy=2))
        send(ref, ref, n_s, n_r.at[1], dev(dy=-2))
        send(ref, ref, n_s, n_r.at[2], dev(dy=1))
        send(ref, ref, n_s, n_r.at[2], dev(dy=-1))

    def hid_spread(_):
        low, high = HID.at[yi(-2)], HID.at[yi(2)]
        arrived(low, n_r.at[0])
        send(low, low, n_s, n_r.at[2], dev(dy=1))
        send(low, low, n_s, n_r.at[2], dev(dy=2))
        arrived(high, n_r.at[1])
        send(high, high, n_s, n_r.at[2], dev(dy=-1))

    def spread(g):
        low, high = DG.at[g, yi(-2)], DG.at[g, yi(2)]
        arrived(low, d_r.at[g, 0])
        send(low, low, d_s, e_r.at[g], dev(dy=1))
        if g % 2 == 0:
            send(low, low, d_s, e_r.at[g], dev(dy=2))
        arrived(high, d_r.at[g, 1])
        send(high, high, d_s, e_r.at[g], dev(dy=-1))
        if g % 2 == 1:
            send(high, high, d_s, e_r.at[g], dev(dy=-2))

    def back(g):
        arrived(DG.at[g, 0:5], e_r.at[g])
        pair = DG[g].astype(F32).reshape(64 * S, 2 * PAD).astype(BF16)
        DC[g * 64 * S : (g + 1) * 64 * S] = pair
        total = dot(pair, WE[: 2 * PAD], NN).reshape(S, 2, NX, 8, FEATS)
        for s in range(S):
            for k in range(2):
                GTS[g, k, s] = total[s, k]
        send(GTS.at[g, 1 - c], GR.at[g], g_s, g_r.at[g], dev(dc=1))

    def over_x(g):
        arrived(GR.at[g], g_r.at[g])

        def mine(k):
            return jnp.concatenate([GTS[g, c, s, xi(k)] + GR[g, s, xi(k)] for s in range(S)], axis=0)

        for k in (2, 1, 3):
            XS[g, k - 1] = mine(k).astype(BF16)
            send(XS.at[g, k - 1], XR.at[g, k - 1], h_s, h_r.at[g], dev(dx=k))
        KX[g] = mine(0)

    def over_z(g):
        arrived(XR.at[g], h_r.at[g])
        total = KX[g] + XR[g, 0].astype(F32) + XR[g, 1].astype(F32) + XR[g, 2].astype(F32)
        for s, d in enumerate(GROUPS[g]):
            part = total[s * 8 : s * 8 + 8]
            if d == 0:
                ZO[...] = part
            else:
                i = d + 3
                ZS[i] = part
                send(ZS.at[i], ZR.at[i], k_s, k_r.at[0], dev(dz=d))

    def weights(i, left, right, out):
        out[...] = (dot(left, right[...], TN)[:UNITS] * KEEP[i].astype(F32)).astype(BF16)

    def pair_weights(_):
        weights(0, DC[:, :PAD], TOKS, o_g)
        weights(1, DC[:, PAD:], TOKS, o_u)

    def down_weights(_):
        arrived(HID.at[0:5], n_r.at[2])
        hidden = jnp.concatenate(
            [HID[:, g].astype(F32).reshape(64 * S, PAD) for g in range(N)], axis=0
        ).astype(BF16)
        weights(2, hidden, GRDS, o_d)

    stages = (
        fwd, slab, prep, partial, relay, owned, spread, back, over_x, over_z,
        hid, hid_spread, pair_weights, down_weights,
    )
    for stage, at in ORDER:
        stages[stage](at)
    arrived(ZR.at[0:7], k_r.at[0])
    total = ZO[...]
    for d in (1, -1, 2, -2, 3, -3, 4):
        total = total + ZR[d + 3]
    o_t[...] = total.astype(BF16)
    for ref, ssem in (
        (G.at[0:3, :, 0:3], x_s), (G.at[0:5, 0, 0], z_s), (G.at[0:5], c_s), (S1, y1_s), (S3, y2_s),
        (DG.at[:, 0:7], d_s), (GTS.at[:, 0], g_s), (XS, h_s), (ZS.at[0:7], k_s), (HID.at[0:7], n_s),
    ):
        left(ref, ssem)


def store(a, b, c, d, oa, ob, oc, od, sem):
    copies = [
        pltpu.make_async_copy(s, t, sem.at[i])
        for i, (s, t) in enumerate(((a, oa), (b, ob), (c, oc), (d, od)))
    ]
    for cp in copies:
        cp.start()
    for cp in copies:
        cp.wait()


def shards(tokens, out_grad, w_gate, w_up, w_down, mask_gate, mask_up, mask_down):
    vm = pltpu.VMEM
    dma = pltpu.SemaphoreType.DMA
    scratch = [
        vm((8, FEATS), BF16), vm((8, FEATS), BF16), vm((3, UNITS, FEATS), BF16),
        vm((3,) + mask_gate.shape[::-1], jnp.int32),
        vm((NZ, 2, NX, 16, FEATS), BF16), vm((WIDE, FEATS), BF16), vm((FEATS, WIDE), BF16),
        vm((3, UNITS, FEATS), BF16),
        vm((TOKENS, FEATS), BF16), vm((TOKENS, FEATS), BF16), vm((N, NY, RO, WIDE), F32),
        vm((N, 5, RO, WIDE), BF16), vm((N, 5, RO, WIDE), BF16), vm((N, 2, RO, WIDE), BF16), vm((N, 2, RO, WIDE), BF16),
        vm((N, NY, RO, 2 * PAD), BF16), vm((TOKENS, 2 * PAD), BF16), vm((NY, N, RO, PAD), BF16),
        vm((N, 2, S, NX, 8, FEATS), F32), vm((N, S, NX, 8, FEATS), F32),
        vm((N, 3, RO, FEATS), BF16), vm((N, 3, RO, FEATS), BF16), vm((N, RO, FEATS), F32),
        vm((8, 8, FEATS), F32), vm((8, 8, FEATS), F32), vm((8, FEATS), F32),
        dma((8,)),
        dma((10,)), dma((8,)), dma((8,)), dma((8,)), dma((N,)), dma((N,)), dma((N, 2)), dma((N,)),
        dma((N,)), dma((N,)), dma((1,)), dma((3,)),
    ]
    outs = [jax.ShapeDtypeStruct(tokens.shape, BF16)] + [
        jax.ShapeDtypeStruct(w_gate.shape, BF16) for _ in range(3)
    ]
    operands = [
        pltpu.with_memory_space_constraint(a, pltpu.HBM)
        for a in (tokens, out_grad, w_gate, w_up, w_down, mask_gate.T, mask_up.T, mask_down.T)
    ]
    results = pl.pallas_call(
        kernel,
        out_shape=outs,
        in_specs=[pl.BlockSpec(memory_space=pltpu.HBM)] * 8,
        out_specs=[pl.BlockSpec(memory_space=pltpu.VMEM)] * 4,
        scratch_shapes=scratch,
        compiler_params=pltpu.CompilerParams(
            collective_id=0, has_side_effects=True, vmem_limit_bytes=40 * 1024 * 1024
        ),
        name="ffn_backward",
    )(*operands)
    return pl.pallas_call(
        store,
        out_shape=outs,
        in_specs=[pl.BlockSpec(memory_space=pltpu.VMEM)] * 4,
        out_specs=[pl.BlockSpec(memory_space=pltpu.HBM)] * 4,
        scratch_shapes=[dma((4,))],
        compiler_params=pltpu.CompilerParams(vmem_limit_bytes=8 * 1024 * 1024),
        name="store_results",
    )(*results)


def solution(mesh):
    spec = P("row", "col")
    return jax.shard_map(
        shards,
        mesh=mesh,
        in_specs=(spec,) * 5 + (P(),) * 3,
        out_specs=(spec,) * 4,
        check_vma=False,
    )
```

```python
import jax
import jax.numpy as jnp
from jax import lax
from jax.experimental import pallas as pl
from jax.experimental.pallas import tpu as pltpu
from jax.sharding import PartitionSpec as P

NZ, NX, NY = 8, 4, 8
UNITS, FEATS, PAD = 224, 1024, 256
WIDE = 3 * PAD
TOKENS = 512
GROUPS = ((0,), (4,), (1,), (-1,), (3,), (-3,), (2,), (-2,))
N, S = len(GROUPS), len(GROUPS[0])
SLABS = tuple(o for g in GROUPS for o in g)
RO = 8 * S
F32, BF16 = jnp.float32, jnp.bfloat16
NN = (((1,), (0,)), ((), ()))
NT = (((1,), (1,)), ((), ()))
TN = (((0,), (0,)), ((), ()))


ORDER = (
    (2, 0), (2, 1), (2, 2), (1, 0), (0, 4), (3, 0), (0, 3), (0, -3), (0, 2), (0, -2),
    (1, 4), (4, 0), (1, 1), (1, -1), (3, 1), (1, 3), (3, 2), (3, 3), (1, -3), (3, 4),
    (5, 0), (1, 2), (3, 5), (4, 1), (1, -2), (3, 6), (4, 2), (4, 3), (3, 7), (4, 4),
    (6, 0), (4, 5), (5, 1), (4, 6), (5, 2), (5, 3), (4, 7), (5, 4), (7, 0), (5, 5),
    (6, 1), (5, 6), (6, 2), (8, 0), (6, 3), (5, 7), (6, 4), (6, 5), (7, 1), (6, 6),
    (9, 0), (7, 2), (7, 3), (6, 7), (8, 1), (7, 4), (8, 2), (7, 5), (8, 3), (7, 6),
    (8, 4), (10, 0), (8, 5), (9, 1), (7, 7), (8, 6), (9, 2), (8, 7), (9, 3),
    (9, 4), (9, 5), (11, 0), (9, 6), (9, 7), (12, 0), (13, 0),
)


def dot(a, b, dims):
    return lax.dot_general(a, b, dims, preferred_element_type=F32)


def expand(mask, row_start, col_start):
    wide, blocks = mask.shape
    unit = (row_start + lax.broadcasted_iota(jnp.int32, (UNITS, blocks), 0)) >> 7
    left = (unit == lax.broadcasted_iota(jnp.int32, (UNITS, blocks), 1)).astype(F32).astype(BF16)
    feat = (col_start + lax.broadcasted_iota(jnp.int32, (wide, FEATS), 1)) >> 7
    right = (feat == lax.broadcasted_iota(jnp.int32, (wide, FEATS), 0)).astype(F32).astype(BF16)
    inner = dot(left, mask.astype(F32).astype(BF16), NT)
    return dot(inner.astype(BF16), right, NN)


def kernel(
    tok, grd, wg, wu, wd, mg, mu, md,
    o_t, o_g, o_u, o_d,
    tokv, grdv, wv, mv, G, WE, WT, KEEP, TOKS, GRDS, P32,
    S1, R1, S3, R3, DG, DC, HID, GTS, GR, XS, XR, KX, ZS, ZR, ZO,
    lsem, out_sem, x_r, z_r, c_r, y1_r, y2_r, d_r, e_r, g_r, h_r, k_r, n_r,
):
    row, y = lax.axis_index("row"), lax.axis_index("col")
    c = lax.rem(row, 2)
    x = lax.rem(row // 2, NX)
    z = row // (2 * NX)

    def zi(d):
        return lax.rem(z + (d + NZ), NZ)

    def xi(d):
        return lax.rem(x + (d + NX), NX)

    def yi(d):
        return lax.rem(y + (d + NY), NY)

    def dev(dz=0, dx=0, dc=0, dy=0):
        return ((zi(dz) * NX + xi(dx)) * 2 + lax.rem(c + dc, 2), yi(dy))

    x_s, z_s, c_s, y1_s, y2_s, d_s, g_s, h_s, k_s, n_s = (out_sem.at[i] for i in range(10))

    def copy(src, dst, ssem, rsem, where):
        return pltpu.make_async_remote_copy(
            src, dst, ssem, rsem, device_id=where, device_id_type=pl.DeviceIdType.MESH
        )

    def send(src, dst, ssem, rsem, where):
        copy(src, dst, ssem, rsem, where).start()

    def arrived(ref, rsem):
        copy(ref, ref, out_sem.at[0], rsem, dev(dc=1)).wait_recv()

    def left(ref, ssem):
        copy(ref, ref, ssem, k_r.at[0], dev(dc=1)).wait_send()

    loads = [
        pltpu.make_async_copy(s, d, lsem.at[i])
        for i, (s, d) in enumerate(
            (
                (tok, tokv), (grd, grdv),
                (mg, mv.at[0]), (mu, mv.at[1]), (md, mv.at[2]),
                (wg, wv.at[0]), (wu, wv.at[1]), (wd, wv.at[2]),
            )
        )
    ]
    loads[0].start()
    loads[1].start()
    peers = (
        [dev(dz=k) for k in (4, 3, -3, 2, -2, 1, -1)]
        + [dev(dx=k) for k in (2, 1, 3)]
        + [dev(dy=k) for k in (2, -2, 1, -1)]
        + [dev(dc=1)]
    )
    barrier = pltpu.get_barrier_semaphore()
    for p in peers:
        pl.semaphore_signal(barrier, inc=1, device_id=p, device_id_type=pl.DeviceIdType.MESH)
    for cp in loads[2:]:
        cp.start()
    loads[0].wait()
    loads[1].wait()
    G[z, c, x] = jnp.concatenate([tokv[...].astype(F32), grdv[...].astype(F32)], axis=0).astype(BF16)
    pl.semaphore_wait(barrier, len(peers))

    def over(o):
        ref = G.at[zi(o), c, x]
        for k in (1, 3, 2):
            send(ref, ref, x_s, x_r.at[o + 3], dev(dx=k))

    def fwd(o):
        i = (-o if o < 4 else 4) + 3
        arrived(G.at[zi(o), c, x], z_r.at[i])
        over(o)

    def slab(o):
        ref = G.at[zi(o), c]
        if abs(o) == 1:
            arrived(ref, z_r.at[3 - o])
        else:
            arrived(G.at[zi(o), c, 0:3], x_r.at[o + 3])
        send(ref, ref, c_s, c_r.at[o + 3], dev(dc=1))
        if o == 0:
            for d in (1, -1):
                send(ref, ref, c_s, z_r.at[d + 3], dev(dz=d))

    own = G.at[z, c, x]
    over(0)
    for d in (4, -3, 3, -2, 2):
        send(own, own, z_s, z_r.at[d + 3], dev(dz=d))

    def prep(i):
        loads[2 + i].wait()
        loads[5 + i].wait()
        keep = expand(mv[i], row * UNITS, y * FEATS)
        KEEP[i] = keep.astype(BF16)
        eff = jnp.concatenate(
            [(wv[i].astype(F32) * keep).astype(BF16), jnp.zeros((PAD - UNITS, FEATS), BF16)], axis=0
        )
        WE[i * PAD : (i + 1) * PAD] = eff
        WT[:, i * PAD : (i + 1) * PAD] = eff.T

    def partial(g):
        toks, grds = [], []
        for o in GROUPS[g]:
            arrived(G.at[zi(o), 1 - c], c_r.at[o + 3])
            v = G[zi(o)].astype(F32)
            toks.append(v[:, :, :8].reshape(64, FEATS))
            grds.append(v[:, :, 8:].reshape(64, FEATS))
        t = jnp.concatenate(toks, axis=0).astype(BF16)
        r = jnp.concatenate(grds, axis=0).astype(BF16)
        at = slice(g * 64 * S, (g + 1) * 64 * S)
        TOKS[at] = t
        GRDS[at] = r
        P32[g, :, :, : 2 * PAD] = dot(t, WT[:, : 2 * PAD], NN).reshape(NY, RO, 2 * PAD)
        P32[g, :, :, 2 * PAD :] = dot(r, WT[:, 2 * PAD :], NN).reshape(NY, RO, PAD)
        for i, k in enumerate((1, 3, -1, -3, 4)):
            S1[g, i] = P32[g, yi(k)].astype(BF16)
        send(S1.at[g, 0:2], R1.at[g, 0:2], y1_s, y1_r.at[g], dev(dy=1))
        send(S1.at[g, 2:4], R1.at[g, 2:4], y1_s, y1_r.at[g], dev(dy=-1))
        send(S1.at[g, 4], R1.at[g, 4], y1_s, y1_r.at[g], dev(dy=2 if g % 2 == 0 else -2))

    def relay(g):
        arrived(R1.at[g], y1_r.at[g])
        up = P32[g, yi(2)] + R1[g, 1].astype(F32)
        down = P32[g, yi(-2)] + R1[g, 3].astype(F32)
        far = R1[g, 4].astype(F32)
        if g % 2 == 0:
            up = up + far
        else:
            down = down + far
        S3[g, 0] = up.astype(BF16)
        send(S3.at[g, 0], R3.at[g, 0], y2_s, y2_r.at[g], dev(dy=2))
        S3[g, 1] = down.astype(BF16)
        send(S3.at[g, 1], R3.at[g, 1], y2_s, y2_r.at[g], dev(dy=-2))

    def owned(g):
        arrived(R3.at[g], y2_r.at[g])
        total = (
            P32[g, y]
            + (R1[g, 0].astype(F32) + R1[g, 2].astype(F32))
            + (R3[g, 0].astype(F32) + R3[g, 1].astype(F32))
        )
        gate, upper, dhid = total[:, :PAD], total[:, PAD : 2 * PAD], total[:, 2 * PAD :]
        sig = jax.nn.sigmoid(gate)
        act = gate * sig
        dgate = dhid * upper * sig * (1.0 + gate * (1.0 - sig))
        DG[g, y] = jnp.concatenate([dgate, dhid * act], axis=1).astype(BF16)
        ref = DG.at[g, y]
        send(ref, ref, d_s, d_r.at[g, 0], dev(dy=2))
        send(ref, ref, d_s, d_r.at[g, 1], dev(dy=-2))
        send(ref, ref, d_s, e_r.at[g], dev(dy=1))
        send(ref, ref, d_s, e_r.at[g], dev(dy=-1))
        HID[y, g] = (act * upper).astype(BF16)

    def hid(_):
        ref = HID.at[y]
        send(ref, ref, n_s, n_r.at[0], dev(dy=2))
        send(ref, ref, n_s, n_r.at[1], dev(dy=-2))
        send(ref, ref, n_s, n_r.at[2], dev(dy=1))
        send(ref, ref, n_s, n_r.at[2], dev(dy=-1))

    def hid_spread(_):
        low, high = HID.at[yi(-2)], HID.at[yi(2)]
        arrived(low, n_r.at[0])
        send(low, low, n_s, n_r.at[2], dev(dy=1))
        send(low, low, n_s, n_r.at[2], dev(dy=2))
        arrived(high, n_r.at[1])
        send(high, high, n_s, n_r.at[2], dev(dy=-1))

    def spread(g):
        low, high = DG.at[g, yi(-2)], DG.at[g, yi(2)]
        arrived(low, d_r.at[g, 0])
        send(low, low, d_s, e_r.at[g], dev(dy=1))
        if g % 2 == 0:
            send(low, low, d_s, e_r.at[g], dev(dy=2))
        arrived(high, d_r.at[g, 1])
        send(high, high, d_s, e_r.at[g], dev(dy=-1))
        if g % 2 == 1:
            send(high, high, d_s, e_r.at[g], dev(dy=-2))

    def back(g):
        arrived(DG.at[g, 0:5], e_r.at[g])
        pair = DG[g].astype(F32).reshape(64 * S, 2 * PAD).astype(BF16)
        DC[g * 64 * S : (g + 1) * 64 * S] = pair
        total = dot(pair, WE[: 2 * PAD], NN).reshape(S, 2, NX, 8, FEATS)
        for s in range(S):
            for k in range(2):
                GTS[g, k, s] = total[s, k]
        send(GTS.at[g, 1 - c], GR.at[g], g_s, g_r.at[g], dev(dc=1))

    def over_x(g):
        arrived(GR.at[g], g_r.at[g])

        def mine(k):
            return jnp.concatenate([GTS[g, c, s, xi(k)] + GR[g, s, xi(k)] for s in range(S)], axis=0)

        for k in (2, 1, 3):
            XS[g, k - 1] = mine(k).astype(BF16)
            send(XS.at[g, k - 1], XR.at[g, k - 1], h_s, h_r.at[g], dev(dx=k))
        KX[g] = mine(0)

    def over_z(g):
        arrived(XR.at[g], h_r.at[g])
        total = KX[g] + XR[g, 0].astype(F32) + XR[g, 1].astype(F32) + XR[g, 2].astype(F32)
        for s, d in enumerate(GROUPS[g]):
            part = total[s * 8 : s * 8 + 8]
            if d == 0:
                ZO[...] = part
            else:
                i = d + 3
                ZS[i] = part
                send(ZS.at[i], ZR.at[i], k_s, k_r.at[0], dev(dz=d))

    def weights(i, left, right, out):
        out[...] = (dot(left, right[...], TN)[:UNITS] * KEEP[i].astype(F32)).astype(BF16)

    def pair_weights(_):
        weights(0, DC[:, :PAD], TOKS, o_g)
        weights(1, DC[:, PAD:], TOKS, o_u)

    def down_weights(_):
        arrived(HID.at[0:5], n_r.at[2])
        hidden = jnp.concatenate(
            [HID[:, g].astype(F32).reshape(64 * S, PAD) for g in range(N)], axis=0
        ).astype(BF16)
        weights(2, hidden, GRDS, o_d)

    stages = (
        fwd, slab, prep, partial, relay, owned, spread, back, over_x, over_z,
        hid, hid_spread, pair_weights, down_weights,
    )
    for stage, at in ORDER:
        stages[stage](at)
    arrived(ZR.at[0:7], k_r.at[0])
    total = ZO[...]
    for d in (1, -1, 2, -2, 3, -3, 4):
        total = total + ZR[d + 3]
    o_t[...] = total.astype(BF16)
    for ref, ssem in (
        (G.at[0:3, :, 0:3], x_s), (G.at[0:5, 0, 0], z_s), (G.at[0:5], c_s), (S1, y1_s), (S3, y2_s),
        (DG.at[:, 0:7], d_s), (GTS.at[:, 0], g_s), (XS, h_s), (ZS.at[0:7], k_s), (HID.at[0:7], n_s),
    ):
        left(ref, ssem)


def store(a, b, c, d, oa, ob, oc, od, sem):
    copies = [
        pltpu.make_async_copy(s, t, sem.at[i])
        for i, (s, t) in enumerate(((a, oa), (b, ob), (c, oc), (d, od)))
    ]
    for cp in copies:
        cp.start()
    for cp in copies:
        cp.wait()


def shards(tokens, out_grad, w_gate, w_up, w_down, mask_gate, mask_up, mask_down):
    vm = pltpu.VMEM
    dma = pltpu.SemaphoreType.DMA
    scratch = [
        vm((8, FEATS), BF16), vm((8, FEATS), BF16), vm((3, UNITS, FEATS), BF16),
        vm((3,) + mask_gate.shape[::-1], jnp.int32),
        vm((NZ, 2, NX, 16, FEATS), BF16), vm((WIDE, FEATS), BF16), vm((FEATS, WIDE), BF16),
        vm((3, UNITS, FEATS), BF16),
        vm((TOKENS, FEATS), BF16), vm((TOKENS, FEATS), BF16), vm((N, NY, RO, WIDE), F32),
        vm((N, 5, RO, WIDE), BF16), vm((N, 5, RO, WIDE), BF16), vm((N, 2, RO, WIDE), BF16), vm((N, 2, RO, WIDE), BF16),
        vm((N, NY, RO, 2 * PAD), BF16), vm((TOKENS, 2 * PAD), BF16), vm((NY, N, RO, PAD), BF16),
        vm((N, 2, S, NX, 8, FEATS), F32), vm((N, S, NX, 8, FEATS), F32),
        vm((N, 3, RO, FEATS), BF16), vm((N, 3, RO, FEATS), BF16), vm((N, RO, FEATS), F32),
        vm((8, 8, FEATS), F32), vm((8, 8, FEATS), F32), vm((8, FEATS), F32),
        dma((8,)),
        dma((10,)), dma((8,)), dma((8,)), dma((8,)), dma((N,)), dma((N,)), dma((N, 2)), dma((N,)),
        dma((N,)), dma((N,)), dma((1,)), dma((3,)),
    ]
    outs = [jax.ShapeDtypeStruct(tokens.shape, BF16)] + [
        jax.ShapeDtypeStruct(w_gate.shape, BF16) for _ in range(3)
    ]
    operands = [
        pltpu.with_memory_space_constraint(a, pltpu.HBM)
        for a in (tokens, out_grad, w_gate, w_up, w_down, mask_gate.T, mask_up.T, mask_down.T)
    ]
    results = pl.pallas_call(
        kernel,
        out_shape=outs,
        in_specs=[pl.BlockSpec(memory_space=pltpu.HBM)] * 8,
        out_specs=[pl.BlockSpec(memory_space=pltpu.VMEM)] * 4,
        scratch_shapes=scratch,
        compiler_params=pltpu.CompilerParams(
            collective_id=0, has_side_effects=True, vmem_limit_bytes=40 * 1024 * 1024
        ),
        name="ffn_backward",
    )(*operands)
    return pl.pallas_call(
        store,
        out_shape=outs,
        in_specs=[pl.BlockSpec(memory_space=pltpu.VMEM)] * 4,
        out_specs=[pl.BlockSpec(memory_space=pltpu.HBM)] * 4,
        scratch_shapes=[dma((4,))],
        compiler_params=pltpu.CompilerParams(vmem_limit_bytes=8 * 1024 * 1024),
        name="store_results",
    )(*results)


def solution(mesh):
    spec = P("row", "col")
    return jax.shard_map(
        shards,
        mesh=mesh,
        in_specs=(spec,) * 5 + (P(),) * 3,
        out_specs=(spec,) * 4,
        check_vma=False,
    )
```

```python
import jax
import jax.numpy as jnp
from jax import lax
from jax.experimental import pallas as pl
from jax.experimental.pallas import tpu as pltpu
from jax.sharding import PartitionSpec as P

NZ, NX, NY = 8, 4, 8
UNITS, FEATS, PAD = 224, 1024, 256
WIDE = 3 * PAD
TOKENS = 512
GROUPS = ((0,), (4,), (1,), (-1,), (3,), (-3,), (2,), (-2,))
N, S = len(GROUPS), len(GROUPS[0])
SLABS = tuple(o for g in GROUPS for o in g)
RO = 8 * S
F32, BF16 = jnp.float32, jnp.bfloat16
NN = (((1,), (0,)), ((), ()))
NT = (((1,), (1,)), ((), ()))
TN = (((0,), (0,)), ((), ()))


ORDER = (
    (2, 0), (2, 1), (2, 2), (1, 0), (0, 4), (3, 0), (0, 3), (0, -3), (0, 2), (0, -2),
    (1, 4), (4, 0), (1, 1), (1, -1), (3, 1), (1, 3), (3, 2), (3, 3), (1, -3), (3, 4),
    (5, 0), (1, 2), (3, 5), (4, 1), (1, -2), (3, 6), (4, 2), (4, 3), (3, 7), (4, 4),
    (6, 0), (4, 5), (5, 1), (4, 6), (5, 2), (5, 3), (4, 7), (5, 4), (7, 0), (5, 5),
    (6, 1), (5, 6), (6, 2), (8, 0), (6, 3), (5, 7), (6, 4), (6, 5), (7, 1), (6, 6),
    (9, 0), (7, 2), (7, 3), (6, 7), (8, 1), (7, 4), (8, 2), (7, 5), (8, 3), (7, 6),
    (8, 4), (10, 0), (8, 5), (9, 1), (7, 7), (8, 6), (9, 2), (12, 0), (8, 7), (9, 3),
    (9, 4), (9, 5), (11, 0), (9, 6), (9, 7), (13, 0),
)


def dot(a, b, dims):
    return lax.dot_general(a, b, dims, preferred_element_type=F32)


def expand(mask, row_start, col_start):
    wide, blocks = mask.shape
    unit = (row_start + lax.broadcasted_iota(jnp.int32, (UNITS, blocks), 0)) >> 7
    left = (unit == lax.broadcasted_iota(jnp.int32, (UNITS, blocks), 1)).astype(F32).astype(BF16)
    feat = (col_start + lax.broadcasted_iota(jnp.int32, (wide, FEATS), 1)) >> 7
    right = (feat == lax.broadcasted_iota(jnp.int32, (wide, FEATS), 0)).astype(F32).astype(BF16)
    inner = dot(left, mask.astype(F32).astype(BF16), NT)
    return dot(inner.astype(BF16), right, NN)


def kernel(
    tok, grd, wg, wu, wd, mg, mu, md,
    o_t, o_g, o_u, o_d,
    tokv, grdv, wv, mv, G, WE, WT, KEEP, TOKS, GRDS, P32,
    S1, R1, S3, R3, DG, DC, HID, GTS, GR, XS, XR, KX, ZS, ZR, ZO,
    lsem, out_sem, x_r, z_r, c_r, y1_r, y2_r, d_r, e_r, g_r, h_r, k_r, n_r,
):
    row, y = lax.axis_index("row"), lax.axis_index("col")
    c = lax.rem(row, 2)
    x = lax.rem(row // 2, NX)
    z = row // (2 * NX)

    def zi(d):
        return lax.rem(z + (d + NZ), NZ)

    def xi(d):
        return lax.rem(x + (d + NX), NX)

    def yi(d):
        return lax.rem(y + (d + NY), NY)

    def dev(dz=0, dx=0, dc=0, dy=0):
        return ((zi(dz) * NX + xi(dx)) * 2 + lax.rem(c + dc, 2), yi(dy))

    x_s, z_s, c_s, y1_s, y2_s, d_s, g_s, h_s, k_s, n_s = (out_sem.at[i] for i in range(10))

    def copy(src, dst, ssem, rsem, where):
        return pltpu.make_async_remote_copy(
            src, dst, ssem, rsem, device_id=where, device_id_type=pl.DeviceIdType.MESH
        )

    def send(src, dst, ssem, rsem, where):
        copy(src, dst, ssem, rsem, where).start()

    def arrived(ref, rsem):
        copy(ref, ref, out_sem.at[0], rsem, dev(dc=1)).wait_recv()

    def left(ref, ssem):
        copy(ref, ref, ssem, k_r.at[0], dev(dc=1)).wait_send()

    loads = [
        pltpu.make_async_copy(s, d, lsem.at[i])
        for i, (s, d) in enumerate(
            (
                (tok, tokv), (grd, grdv),
                (mg, mv.at[0]), (mu, mv.at[1]), (md, mv.at[2]),
                (wg, wv.at[0]), (wu, wv.at[1]), (wd, wv.at[2]),
            )
        )
    ]
    loads[0].start()
    loads[1].start()
    peers = (
        [dev(dz=k) for k in (4, 3, -3, 2, -2, 1, -1)]
        + [dev(dx=k) for k in (2, 1, 3)]
        + [dev(dy=k) for k in (2, -2, 1, -1)]
        + [dev(dc=1)]
    )
    barrier = pltpu.get_barrier_semaphore()
    for p in peers:
        pl.semaphore_signal(barrier, inc=1, device_id=p, device_id_type=pl.DeviceIdType.MESH)
    for cp in loads[2:]:
        cp.start()
    loads[0].wait()
    loads[1].wait()
    G[z, c, x] = jnp.concatenate([tokv[...].astype(F32), grdv[...].astype(F32)], axis=0).astype(BF16)
    pl.semaphore_wait(barrier, len(peers))

    def over(o):
        ref = G.at[zi(o), c, x]
        for k in (1, 3, 2):
            send(ref, ref, x_s, x_r.at[o + 3], dev(dx=k))

    def fwd(o):
        i = (-o if o < 4 else 4) + 3
        arrived(G.at[zi(o), c, x], z_r.at[i])
        over(o)

    def slab(o):
        ref = G.at[zi(o), c]
        if abs(o) == 1:
            arrived(ref, z_r.at[3 - o])
        else:
            arrived(G.at[zi(o), c, 0:3], x_r.at[o + 3])
        send(ref, ref, c_s, c_r.at[o + 3], dev(dc=1))
        if o == 0:
            for d in (1, -1):
                send(ref, ref, c_s, z_r.at[d + 3], dev(dz=d))

    own = G.at[z, c, x]
    over(0)
    for d in (4, -3, 3, -2, 2):
        send(own, own, z_s, z_r.at[d + 3], dev(dz=d))

    def prep(i):
        loads[2 + i].wait()
        loads[5 + i].wait()
        keep = expand(mv[i], row * UNITS, y * FEATS)
        KEEP[i] = keep.astype(BF16)
        eff = jnp.concatenate(
            [(wv[i].astype(F32) * keep).astype(BF16), jnp.zeros((PAD - UNITS, FEATS), BF16)], axis=0
        )
        WE[i * PAD : (i + 1) * PAD] = eff
        WT[:, i * PAD : (i + 1) * PAD] = eff.T

    def partial(g):
        toks, grds = [], []
        for o in GROUPS[g]:
            arrived(G.at[zi(o), 1 - c], c_r.at[o + 3])
            v = G[zi(o)].astype(F32)
            toks.append(v[:, :, :8].reshape(64, FEATS))
            grds.append(v[:, :, 8:].reshape(64, FEATS))
        t = jnp.concatenate(toks, axis=0).astype(BF16)
        r = jnp.concatenate(grds, axis=0).astype(BF16)
        at = slice(g * 64 * S, (g + 1) * 64 * S)
        TOKS[at] = t
        GRDS[at] = r
        P32[g, :, :, : 2 * PAD] = dot(t, WT[:, : 2 * PAD], NN).reshape(NY, RO, 2 * PAD)
        P32[g, :, :, 2 * PAD :] = dot(r, WT[:, 2 * PAD :], NN).reshape(NY, RO, PAD)
        S1[g, 4] = P32[g, yi(4)].astype(BF16)
        send(S1.at[g, 4], R1.at[g, 4], y1_s, y1_r.at[g], dev(dy=2 if g % 2 == 0 else -2))
        for i, way in ((0, 1), (2, -1)):
            S1[g, i] = P32[g, yi(way)].astype(BF16)
            S1[g, i + 1] = P32[g, yi(3 * way)].astype(BF16)
            send(S1.at[g, i : i + 2], R1.at[g, i : i + 2], y1_s, y1_r.at[g], dev(dy=way))

    def relay(g):
        arrived(R1.at[g], y1_r.at[g])
        up = P32[g, yi(2)] + R1[g, 1].astype(F32)
        down = P32[g, yi(-2)] + R1[g, 3].astype(F32)
        far = R1[g, 4].astype(F32)
        if g % 2 == 0:
            up = up + far
        else:
            down = down + far
        S3[g, 0] = up.astype(BF16)
        send(S3.at[g, 0], R3.at[g, 0], y2_s, y2_r.at[g], dev(dy=2))
        S3[g, 1] = down.astype(BF16)
        send(S3.at[g, 1], R3.at[g, 1], y2_s, y2_r.at[g], dev(dy=-2))

    def owned(g):
        arrived(R3.at[g], y2_r.at[g])
        total = (
            P32[g, y]
            + (R1[g, 0].astype(F32) + R1[g, 2].astype(F32))
            + (R3[g, 0].astype(F32) + R3[g, 1].astype(F32))
        )
        gate, upper, dhid = total[:, :PAD], total[:, PAD : 2 * PAD], total[:, 2 * PAD :]
        sig = jax.nn.sigmoid(gate)
        act = gate * sig
        dgate = dhid * upper * sig * (1.0 + gate * (1.0 - sig))
        DG[g, y] = jnp.concatenate([dgate, dhid * act], axis=1).astype(BF16)
        ref = DG.at[g, y]
        send(ref, ref, d_s, d_r.at[g, 0], dev(dy=2))
        send(ref, ref, d_s, d_r.at[g, 1], dev(dy=-2))
        send(ref, ref, d_s, e_r.at[g], dev(dy=1))
        send(ref, ref, d_s, e_r.at[g], dev(dy=-1))
        HID[y, g] = (act * upper).astype(BF16)

    def hid(_):
        ref = HID.at[y]
        send(ref, ref, n_s, n_r.at[0], dev(dy=2))
        send(ref, ref, n_s, n_r.at[1], dev(dy=-2))
        send(ref, ref, n_s, n_r.at[2], dev(dy=1))
        send(ref, ref, n_s, n_r.at[2], dev(dy=-1))

    def hid_spread(_):
        low, high = HID.at[yi(-2)], HID.at[yi(2)]
        arrived(low, n_r.at[0])
        send(low, low, n_s, n_r.at[2], dev(dy=1))
        send(low, low, n_s, n_r.at[2], dev(dy=2))
        arrived(high, n_r.at[1])
        send(high, high, n_s, n_r.at[2], dev(dy=-1))

    def spread(g):
        low, high = DG.at[g, yi(-2)], DG.at[g, yi(2)]
        arrived(low, d_r.at[g, 0])
        send(low, low, d_s, e_r.at[g], dev(dy=1))
        if g % 2 == 0:
            send(low, low, d_s, e_r.at[g], dev(dy=2))
        arrived(high, d_r.at[g, 1])
        send(high, high, d_s, e_r.at[g], dev(dy=-1))
        if g % 2 == 1:
            send(high, high, d_s, e_r.at[g], dev(dy=-2))

    def back(g):
        arrived(DG.at[g, 0:5], e_r.at[g])
        pair = DG[g].astype(F32).reshape(64 * S, 2 * PAD).astype(BF16)
        DC[g * 64 * S : (g + 1) * 64 * S] = pair
        total = dot(pair, WE[: 2 * PAD], NN).reshape(S, 2, NX, 8, FEATS)
        for s in range(S):
            for k in range(2):
                GTS[g, k, s] = total[s, k]
        send(GTS.at[g, 1 - c], GR.at[g], g_s, g_r.at[g], dev(dc=1))

    def over_x(g):
        arrived(GR.at[g], g_r.at[g])

        def mine(k):
            return jnp.concatenate([GTS[g, c, s, xi(k)] + GR[g, s, xi(k)] for s in range(S)], axis=0)

        for k in (2, 1, 3):
            XS[g, k - 1] = mine(k).astype(BF16)
            send(XS.at[g, k - 1], XR.at[g, k - 1], h_s, h_r.at[g], dev(dx=k))
        KX[g] = mine(0)

    def over_z(g):
        arrived(XR.at[g], h_r.at[g])
        total = KX[g] + XR[g, 0].astype(F32) + XR[g, 1].astype(F32) + XR[g, 2].astype(F32)
        for s, d in enumerate(GROUPS[g]):
            part = total[s * 8 : s * 8 + 8]
            if d == 0:
                ZO[...] = part
            else:
                i = d + 3
                ZS[i] = part
                send(ZS.at[i], ZR.at[i], k_s, k_r.at[0], dev(dz=d))

    def weights(i, left, right, out):
        out[...] = (dot(left, right[...], TN)[:UNITS] * KEEP[i].astype(F32)).astype(BF16)

    def pair_weights(_):
        weights(0, DC[:, :PAD], TOKS, o_g)
        weights(1, DC[:, PAD:], TOKS, o_u)

    def down_weights(_):
        arrived(HID.at[0:5], n_r.at[2])
        hidden = jnp.concatenate(
            [HID[:, g].astype(F32).reshape(64 * S, PAD) for g in range(N)], axis=0
        ).astype(BF16)
        weights(2, hidden, GRDS, o_d)

    stages = (
        fwd, slab, prep, partial, relay, owned, spread, back, over_x, over_z,
        hid, hid_spread, pair_weights, down_weights,
    )
    for stage, at in ORDER:
        stages[stage](at)
    arrived(ZR.at[0:7], k_r.at[0])
    total = ZO[...]
    for d in (1, -1, 2, -2, 3, -3, 4):
        total = total + ZR[d + 3]
    o_t[...] = total.astype(BF16)
    for ref, ssem in (
        (G.at[0:3, :, 0:3], x_s), (G.at[0:5, 0, 0], z_s), (G.at[0:5], c_s), (S1, y1_s), (S3, y2_s),
        (DG.at[:, 0:7], d_s), (GTS.at[:, 0], g_s), (XS, h_s), (ZS.at[0:7], k_s), (HID.at[0:7], n_s),
    ):
        left(ref, ssem)


def store(a, b, c, d, oa, ob, oc, od, sem):
    copies = [
        pltpu.make_async_copy(s, t, sem.at[i])
        for i, (s, t) in enumerate(((a, oa), (b, ob), (c, oc), (d, od)))
    ]
    for cp in copies:
        cp.start()
    for cp in copies:
        cp.wait()


def shards(tokens, out_grad, w_gate, w_up, w_down, mask_gate, mask_up, mask_down):
    vm = pltpu.VMEM
    dma = pltpu.SemaphoreType.DMA
    scratch = [
        vm((8, FEATS), BF16), vm((8, FEATS), BF16), vm((3, UNITS, FEATS), BF16),
        vm((3,) + mask_gate.shape[::-1], jnp.int32),
        vm((NZ, 2, NX, 16, FEATS), BF16), vm((WIDE, FEATS), BF16), vm((FEATS, WIDE), BF16),
        vm((3, UNITS, FEATS), BF16),
        vm((TOKENS, FEATS), BF16), vm((TOKENS, FEATS), BF16), vm((N, NY, RO, WIDE), F32),
        vm((N, 5, RO, WIDE), BF16), vm((N, 5, RO, WIDE), BF16), vm((N, 2, RO, WIDE), BF16), vm((N, 2, RO, WIDE), BF16),
        vm((N, NY, RO, 2 * PAD), BF16), vm((TOKENS, 2 * PAD), BF16), vm((NY, N, RO, PAD), BF16),
        vm((N, 2, S, NX, 8, FEATS), F32), vm((N, S, NX, 8, FEATS), F32),
        vm((N, 3, RO, FEATS), BF16), vm((N, 3, RO, FEATS), BF16), vm((N, RO, FEATS), F32),
        vm((8, 8, FEATS), F32), vm((8, 8, FEATS), F32), vm((8, FEATS), F32),
        dma((8,)),
        dma((10,)), dma((8,)), dma((8,)), dma((8,)), dma((N,)), dma((N,)), dma((N, 2)), dma((N,)),
        dma((N,)), dma((N,)), dma((1,)), dma((3,)),
    ]
    outs = [jax.ShapeDtypeStruct(tokens.shape, BF16)] + [
        jax.ShapeDtypeStruct(w_gate.shape, BF16) for _ in range(3)
    ]
    operands = [
        pltpu.with_memory_space_constraint(a, pltpu.HBM)
        for a in (tokens, out_grad, w_gate, w_up, w_down, mask_gate.T, mask_up.T, mask_down.T)
    ]
    results = pl.pallas_call(
        kernel,
        out_shape=outs,
        in_specs=[pl.BlockSpec(memory_space=pltpu.HBM)] * 8,
        out_specs=[pl.BlockSpec(memory_space=pltpu.VMEM)] * 4,
        scratch_shapes=scratch,
        compiler_params=pltpu.CompilerParams(
            collective_id=0, has_side_effects=True, vmem_limit_bytes=40 * 1024 * 1024
        ),
        name="ffn_backward",
    )(*operands)
    return pl.pallas_call(
        store,
        out_shape=outs,
        in_specs=[pl.BlockSpec(memory_space=pltpu.VMEM)] * 4,
        out_specs=[pl.BlockSpec(memory_space=pltpu.HBM)] * 4,
        scratch_shapes=[dma((4,))],
        compiler_params=pltpu.CompilerParams(vmem_limit_bytes=8 * 1024 * 1024),
        name="store_results",
    )(*results)


def solution(mesh):
    spec = P("row", "col")
    return jax.shard_map(
        shards,
        mesh=mesh,
        in_specs=(spec,) * 5 + (P(),) * 3,
        out_specs=(spec,) * 4,
        check_vma=False,
    )
```
